32 devices in a mesh: grp: 4 (over y, x), ctx: 8 (over z, core).
Axes of the slice: x: 2, y: 2, z: 4, core: 2. Of those that a mesh axis runs over, the one named last changes fastest.
Arguments:
- queries: bfloat16 [16384, 1024], P(('grp', 'ctx')), may hold values from -6 to 6
- keys: bfloat16 [16384, 1024], P(('grp', 'ctx')), may hold values from -6 to 6
- values: bfloat16 [16384, 1024], P(('grp', 'ctx')), may hold values from -6 to 6
- level_weights: float32 [13, 8, 16384], P(None, None, ('grp', 'ctx')), may hold values from 0.1 to 1.5
Outputs:
- attended: bfloat16 [16384, 1024], P(('grp', 'ctx'))
The draws below stay inside these ranges and needn't reach their ends.
All inputs are finite; a program needn't handle non-finite values.
Results may differ from the reference program's by a relative error of at most 0.0095.
Values may be sent and summed in bfloat16 or wider, within the bound.
A program may use at most 64 MiB of HBM per device.

```python
import math
import jax
import jax.numpy as jnp
from jax import lax

H = 8
DK = 128
STRETCH = 64
LEVELS = 13
TOK_DEV = 512
TOKENS = 16384
N_GRP = 4
N_CTX = 8


def block_scale(key, dims, cuts, low, top_value):
    gain = 1.0
    for dim, parts in cuts:
        steps = jax.random.uniform(jax.random.fold_in(jax.random.fold_in(key, 6), dim), (parts,), jnp.float32, low / len(cuts), top_value / len(cuts))
        gain = gain * jnp.repeat(jnp.exp(steps), dims[dim] // parts).reshape((-1,) + (1,) * (len(dims) - 1 - dim))
    return gain


def normal_values(own_key, dims, width, reach, split=(), held_as=jnp.bfloat16):
    values = jax.random.normal(own_key, dims, jnp.float32) * width
    if len(split) > 0:
        values = block_scale(own_key, dims, split, -0.22, 0.18) * values
    return jnp.clip(values, min=-reach, max=reach).astype(held_as)


def setup_inputs(seed: int = 0) -> dict:
    seeds = jax.random.split(jax.random.key(seed), 5)
    return {
        "queries": normal_values(seeds[0], (TOKENS, H * DK), 1.0, 6.0, ((0, 32),)),
        "keys": normal_values(seeds[1], (TOKENS, H * DK), 1.0, 6.0, ((0, 32),)),
        "values": normal_values(seeds[2], (TOKENS, H * DK), 1.0, 6.0, ((0, 32),)),
        "level_weights": jnp.clip(jnp.exp(math.log(1.5) - 2.7080502 * jax.random.uniform(seeds[3], (LEVELS, H, TOKENS), jnp.float32) ** block_scale(seeds[3], (LEVELS, H, TOKENS), ((2, 32),), -0.2, 0.2)), 0.1, 1.5),
    }


def level_factor(level_num):
    token_count = STRETCH if level_num == 0 else STRETCH * 2 ** (level_num - 1)
    return 1.0 / math.sqrt(DK * token_count)

def local_part(query_matrix, key_matrix, value_matrix, level_rows):
    row_count = query_matrix.shape[0]
    local_bits = (row_count // STRETCH).bit_length() - 1
    position = jnp.arange(row_count, dtype=jnp.int32)
    block_ids = position // STRETCH
    stretch_xor = jnp.bitwise_xor(block_ids[:, None], block_ids[None, :])
    level_ids = jnp.zeros((row_count, row_count), jnp.int32)
    for bit_num in range(local_bits):
        level_ids = level_ids + (stretch_xor >= 2 ** bit_num).astype(jnp.int32)
    causal = position[:, None] >= position[None, :]
    weight = jnp.zeros((level_rows.shape[1], row_count, row_count), jnp.float32)
    for level_num in range(local_bits + 1):
        picked = jnp.logical_and(level_ids == level_num, causal)
        weight = weight + jnp.where(picked[None], (level_rows[level_num] * level_factor(level_num))[:, :, None], 0.0)
    scores = jnp.einsum('thk,shk->hts', query_matrix.astype(jnp.float32), key_matrix.astype(jnp.float32))
    weighted = (scores * weight).astype(jnp.bfloat16)
    return jnp.einsum('hts,shv->thv', weighted.astype(jnp.float32), value_matrix.astype(jnp.float32))

def reference(queries, keys, values, level_weights):
    device_count = N_GRP * N_CTX
    ctx_bits = N_CTX.bit_length() - 1
    all_bits = device_count.bit_length() - 1
    local_bits = (TOK_DEV // STRETCH).bit_length() - 1
    query_all = queries.reshape(device_count, TOK_DEV, H, DK)
    key_all = keys.reshape(device_count, TOK_DEV, H, DK)
    value_all = values.reshape(device_count, TOK_DEV, H, DK)
    level_all = level_weights.reshape(LEVELS, H, device_count, TOK_DEV).transpose(2, 0, 1, 3)

    def block_state(coupled_rows):
        return jnp.einsum('pdx,pdo->dxo', coupled_rows[0].astype(jnp.float32), coupled_rows[1].astype(jnp.float32)).astype(jnp.bfloat16)
    states = lax.map(block_state, (key_all, value_all))
    tier_sums = []
    present_block = states.astype(jnp.float32)
    for bit_num in range(all_bits):
        tier_sums.append(present_block)
        paired = present_block.reshape(present_block.shape[0] // 2, 2, H, DK, DK)
        present_block = paired[:, 0] + paired[:, 1]
        if bit_num + 1 == ctx_bits:
            present_block = lax.optimization_barrier(present_block.astype(jnp.bfloat16)).astype(jnp.float32)

    def one_block(inputs):
        block_index, query_matrix, key_matrix, value_matrix, level_rows = inputs
        result = local_part(query_matrix, key_matrix, value_matrix, level_rows)
        for bit_num in range(all_bits):
            owner = jnp.right_shift(block_index, bit_num)
            left_index = jnp.maximum(owner - 1, 0).astype(jnp.int32)
            neighbor_block = lax.dynamic_index_in_dim(tier_sums[bit_num], left_index, 0, keepdims=False)
            neighbor_block = jnp.where(owner % 2 == 1, neighbor_block, 0.0).astype(jnp.bfloat16)
            outer_product = jnp.einsum('ryl,ylf->ryf', query_matrix.astype(jnp.float32), neighbor_block.astype(jnp.float32))
            level_num = 1 + local_bits + bit_num
            level_scale = (level_rows[level_num] * level_factor(level_num)).T
            result = result + outer_product * level_scale[:, :, None]
        return result.astype(jnp.bfloat16)
    block_ids = jnp.arange(device_count, dtype=jnp.int32)
    result = lax.map(one_block, (block_ids, query_all, key_all, value_all, level_all))
    return result.reshape(device_count * TOK_DEV, H * DK)
```

```python
import functools
import math

import jax
import jax.numpy as jnp
from jax import lax
from jax.experimental import pallas as pl
from jax.experimental.pallas import tpu as pltpu
from jax.sharding import PartitionSpec as P

DK = 128
STRETCH = 64
SUB = 2 * STRETCH
MESH = pl.DeviceIdType.MESH
LAG = 2


def level_factor(level_num):
    token_count = STRETCH if level_num == 0 else STRETCH * 2 ** (level_num - 1)
    return 1.0 / math.sqrt(DK * token_count)


def dot_nt(a, b):
    return lax.dot_general(a, b, (((1,), (1,)), ((), ())), preferred_element_type=jnp.float32)


def dot_nn(a, b):
    return lax.dot_general(a, b, (((1,), (0,)), ((), ())), preferred_element_type=jnp.float32)


def kernel(
    ctx_bits, grp_bits,
    q_hbm, k_hbm, v_hbm, w_hbm, out_hbm,
    q_buf, k_buf, v_buf, w_buf, w_head, vt_buf, sub_buf, state, sib, run, acc, out_t, out_buf,
    in_sem, w_sem, out_sem, send_sem, fwd_sem, recv_sem,
):
    heads, rows = q_buf.shape[0], q_buf.shape[1]
    half = heads // 2
    count = rows // SUB
    local_bits = (rows // STRETCH).bit_length() - 1
    depth = ctx_bits + grp_bits
    last = depth - 1
    grp = lax.axis_index("grp")
    ctx = lax.axis_index("ctx")
    core = ctx % 2

    def bit(j):
        if j < ctx_bits:
            return (ctx // 2**j) % 2
        return (grp // 2 ** (j - ctx_bits)) % 2

    def partner(j):
        step = 1 - 2 * bit(j)
        if j < ctx_bits:
            return (grp, ctx + step * 2**j)
        return (grp + step * 2 ** (j - ctx_bits), ctx)

    def mine(i):
        return core * half + i

    def other(i):
        return (1 - core) * half + i

    def columns(h):
        return pl.ds(pl.multiple_of(h * DK, DK), DK)

    def fetch(n, h):
        src, dst = ((q_hbm, q_buf), (k_hbm, k_buf), (v_hbm, v_buf))[n]
        return pltpu.make_async_copy(src.at[:, columns(h)], dst.at[h], in_sem.at[n, h])

    def fetch_w():
        return pltpu.make_async_copy(w_hbm, w_buf, w_sem)

    def put(h):
        return pltpu.make_async_copy(out_buf.at[h], out_hbm.at[:, columns(h)], out_sem.at[h])

    def remote(src, j, h, sem, target):
        return pltpu.make_async_remote_copy(
            src_ref=src, dst_ref=sib.at[j, h], send_sem=sem, recv_sem=recv_sem.at[j, h],
            device_id=target, device_id_type=MESH,
        )

    def first_send(h):
        return remote(state.at[h], 0, h, send_sem.at[0, h], partner(0))

    def stage_send(j, i):
        return remote(run.at[j, i], j, mine(i), send_sem.at[j, mine(i)], partner(j))

    def forward(j, i):
        h = mine(i)
        return remote(sib.at[j, h], j, h, fwd_sem.at[j, h], partner(0))

    def arrival(j, h):
        return remote(sib.at[j, h], j, h, send_sem.at[j, h], partner(0))

    def scale(level, h, start, size):
        return w_head[h, level : level + 1, start : start + size]

    barrier = pltpu.get_barrier_semaphore()
    for j in range(depth):
        pl.semaphore_signal(barrier, inc=1, device_id=partner(j), device_id_type=MESH)
    for i in range(half):
        for h in (other(i), mine(i)):
            fetch(1, h).start()
            fetch(2, h).start()
    fetch_w().start()
    for i in range(half):
        for h in (mine(i), other(i)):
            fetch(0, h).start()
    pl.semaphore_wait(barrier, depth)

    def block_sum(h):
        fetch(1, h).wait()
        fetch(2, h).wait()
        vt = v_buf[h].T
        vt_buf[h] = vt
        sums = [
            dot_nn(vt[:, b * SUB : (b + 1) * SUB], k_buf[h, b * SUB : (b + 1) * SUB, :])
            for b in range(count)
        ]
        slot = 0
        while len(sums) > 1:
            for b in range(0, len(sums), 2):
                sub_buf[h, slot] = sums[b].astype(jnp.bfloat16)
                slot += 1
            sums = [sums[b] + sums[b + 1] for b in range(0, len(sums), 2)]
        state[h] = sums[0].astype(jnp.bfloat16)
        first_send(h).start()

    def open_pair(i, carry):
        block_sum(other(i))
        block_sum(mine(i))
        return carry

    lax.fori_loop(0, half, open_pair, 0)
    fetch_w().wait()
    for level in range(1 + local_bits + depth):
        for h in range(heads):
            w_head[h, level : level + 1, :] = w_buf[level, h : h + 1, :] * level_factor(level)

    def local(h):
        fetch(0, h).wait()
        s = lax.broadcasted_iota(jnp.int32, (SUB, SUB), 0)
        t = lax.broadcasted_iota(jnp.int32, (SUB, SUB), 1)
        causal = s <= t
        crossing = jnp.logical_and(s < STRETCH, t >= STRETCH)
        for b in range(count):
            lo = b * SUB
            q = q_buf[h, lo : lo + SUB, :]
            scores = dot_nt(k_buf[h, lo : lo + SUB, :], q)
            weight = jnp.where(
                crossing, scale(1, h, lo, SUB), scale(0, h, lo, SUB)
            )
            weighted = jnp.where(causal, scores * weight, 0.0).astype(jnp.bfloat16)
            total = dot_nn(vt_buf[h, :, lo : lo + SUB], weighted)
            slot = 0
            for level in range(2, local_bits + 1):
                place = b >> (level - 2)
                if place % 2 == 1:
                    total += scale(level, h, lo, SUB) * dot_nt(sub_buf[h, slot + place // 2], q)
                slot += count >> (level - 1)
            out_t[h, :, lo : lo + SUB] = total

    def cross(j, h):
        level = 1 + local_bits + j
        out_t[h] += scale(level, h, 0, rows) * dot_nt(sib[j, h], q_buf[h])

    def finish(h):
        out_buf[h] = out_t[h].astype(jnp.bfloat16).T
        put(h).start()

    def receive(j, i):
        h = mine(i)
        if j == last:
            @pl.when(bit(j) == 1)
            def _():
                arrival(j, h).wait_recv()
        else:
            arrival(j, h).wait_recv()
        if j >= 1:
            @pl.when(bit(j) == 1)
            def _():
                forward(j, i).start()
        if j < last:
            held = state[h].astype(jnp.float32) if j == 0 else acc[i]
            total = held + sib[j, h].astype(jnp.float32)
            rounded = total.astype(jnp.bfloat16)
            run[j + 1, i] = rounded
            acc[i] = rounded.astype(jnp.float32) if j + 1 == ctx_bits else total
            if j + 1 == last:
                @pl.when(bit(j + 1) == 0)
                def _():
                    stage_send(j + 1, i).start()
            else:
                stage_send(j + 1, i).start()

    def wave(w, carry):
        for j in reversed(range(depth)):
            i = w - LAG * j

            @pl.when(jnp.logical_and(i >= 0, i < half))
            def _():
                receive(j, i)

        @pl.when(w < half)
        def _():
            local(mine(w))
            local(other(w))

        for j in range(depth):
            i = w - LAG * j

            @pl.when(jnp.logical_and(jnp.logical_and(i >= 0, i < half), bit(j) == 1))
            def _():
                cross(j, mine(i))

            @pl.when(jnp.logical_and(i >= 1, i < half + 1))
            def _():
                h = other(i - 1)
                if j == 0:
                    arrival(j, h).wait_recv()

                @pl.when(bit(j) == 1)
                def _():
                    if j > 0:
                        arrival(j, h).wait_recv()
                    cross(j, h)

        final = w - LAG * last

        @pl.when(jnp.logical_and(final >= 0, final < half))
        def _():
            finish(mine(final))

        @pl.when(final >= 1)
        def _():
            finish(other(final - 1))

        return carry

    lax.fori_loop(0, LAG * last + half + 1, wave, 0)

    def close(i, carry):
        for h in (mine(i), other(i)):
            first_send(h).wait_send()
            put(h).wait()
        for j in range(1, depth):
            if j == last:
                @pl.when(bit(j) == 0)
                def _():
                    stage_send(j, i).wait_send()
            else:
                stage_send(j, i).wait_send()

            @pl.when(bit(j) == 1)
            def _():
                forward(j, i).wait_send()
        return carry

    lax.fori_loop(0, half, close, 0)


def on_device(ctx_count, grp_count, queries, keys, values, level_weights):
    rows = queries.shape[0]
    heads = level_weights.shape[1]
    count = rows // SUB
    ctx_bits = ctx_count.bit_length() - 1
    grp_bits = grp_count.bit_length() - 1
    depth = ctx_bits + grp_bits
    half = heads // 2
    bf16, f32 = jnp.bfloat16, jnp.float32
    any_spec = pl.BlockSpec(memory_space=pl.ANY)
    return pl.pallas_call(
        functools.partial(kernel, ctx_bits, grp_bits),
        out_shape=jax.ShapeDtypeStruct(queries.shape, bf16),
        in_specs=[any_spec] * 4,
        out_specs=any_spec,
        scratch_shapes=[
            pltpu.VMEM((heads, rows, DK), bf16),
            pltpu.VMEM((heads, rows, DK), bf16),
            pltpu.VMEM((heads, rows, DK), bf16),
            pltpu.VMEM(level_weights.shape, f32),
            pltpu.VMEM((heads, level_weights.shape[0], rows), f32),
            pltpu.VMEM((heads, DK, rows), bf16),
            pltpu.VMEM((heads, count - 1, DK, DK), bf16),
            pltpu.VMEM((heads, DK, DK), bf16),
            pltpu.VMEM((depth, heads, DK, DK), bf16),
            pltpu.VMEM((depth, half, DK, DK), bf16),
            pltpu.VMEM((half, DK, DK), f32),
            pltpu.VMEM((heads, DK, rows), f32),
            pltpu.VMEM((heads, rows, DK), bf16),
            pltpu.SemaphoreType.DMA((3, heads)),
            pltpu.SemaphoreType.DMA,
            pltpu.SemaphoreType.DMA((heads,)),
            pltpu.SemaphoreType.DMA((depth, heads)),
            pltpu.SemaphoreType.DMA((depth, heads)),
            pltpu.SemaphoreType.DMA((depth, heads)),
        ],
        compiler_params=pltpu.CompilerParams(
            collective_id=0, has_side_effects=True, vmem_limit_bytes=40 * 2**20
        ),
        cost_estimate=pl.CostEstimate(
            flops=2 * rows * heads * DK * DK * (9 + depth), bytes_accessed=8 * rows * heads * DK,
            transcendentals=0,
        ),
    )(queries, keys, values, level_weights)


def solution(mesh):
    return jax.shard_map(
        functools.partial(on_device, mesh.shape["ctx"], mesh.shape["grp"]),
        mesh=mesh,
        in_specs=(
            P(("grp", "ctx"), None),
            P(("grp", "ctx"), None),
            P(("grp", "ctx"), None),
            P(None, None, ("grp", "ctx")),
        ),
        out_specs=P(("grp", "ctx"), None),
        check_vma=False,
    )
```

```python
import functools
import math

import jax
import jax.numpy as jnp
from jax import lax
from jax.experimental import pallas as pl
from jax.experimental.pallas import tpu as pltpu
from jax.sharding import PartitionSpec as P

DK = 128
STRETCH = 64
SUB = 2 * STRETCH
RELAYED = 2
MESH = pl.DeviceIdType.MESH


def level_factor(level_num):
    token_count = STRETCH if level_num == 0 else STRETCH * 2 ** (level_num - 1)
    return 1.0 / math.sqrt(DK * token_count)


def dot_nt(a, b):
    return lax.dot_general(a, b, (((1,), (1,)), ((), ())), preferred_element_type=jnp.float32)


def dot_nn(a, b):
    return lax.dot_general(a, b, (((1,), (0,)), ((), ())), preferred_element_type=jnp.float32)


def kernel(
    ctx_bits, grp_bits,
    q_hbm, k_hbm, v_hbm, w_hbm, out_hbm,
    q_buf, k_buf, v_buf, w_buf, w_head, vt_buf, sub_buf, state, sib, run, acc, out_t, out_buf,
    in_sem, w_sem, out_sem, send_sem, fwd_sem, relay_sem, recv_sem,
):
    heads, rows = q_buf.shape[0], q_buf.shape[1]
    half = heads // 2
    count = rows // SUB
    local_bits = (rows // STRETCH).bit_length() - 1
    depth = ctx_bits + grp_bits
    last = depth - 1
    grp = lax.axis_index("grp")
    ctx = lax.axis_index("ctx")
    core = ctx % 2

    def bit(j):
        if j < ctx_bits:
            return (ctx // 2**j) % 2
        return (grp // 2 ** (j - ctx_bits)) % 2

    inner = (bit(1) + bit(2)) % 2

    def partner(j):
        step = 1 - 2 * bit(j)
        if j == RELAYED:
            return (grp, ctx + step * 2)
        if j < ctx_bits:
            return (grp, ctx + step * 2**j)
        return (grp + step * 2 ** (j - ctx_bits), ctx)

    def mine(i):
        return core * half + i

    def other(i):
        return (1 - core) * half + i

    def columns(h):
        return pl.ds(pl.multiple_of(h * DK, DK), DK)

    def fetch(n, h):
        src, dst = ((q_hbm, q_buf), (k_hbm, k_buf), (v_hbm, v_buf))[n]
        return pltpu.make_async_copy(src.at[:, columns(h)], dst.at[h], in_sem.at[n, h])

    def fetch_w():
        return pltpu.make_async_copy(w_hbm, w_buf, w_sem)

    def put(h):
        return pltpu.make_async_copy(out_buf.at[h], out_hbm.at[:, columns(h)], out_sem.at[h])

    def remote(src, j, h, sem, target):
        return pltpu.make_async_remote_copy(
            src_ref=src, dst_ref=sib.at[j, h], send_sem=sem, recv_sem=recv_sem.at[j, h],
            device_id=target, device_id_type=MESH,
        )

    def first_send(h):
        return remote(state.at[h], 0, h, send_sem.at[0, h], partner(0))

    def stage_send(j, i):
        return remote(run.at[j, i], j, mine(i), send_sem.at[j, mine(i)], partner(j))

    def forward(j, i):
        h = mine(i)
        return remote(sib.at[j, h], j, h, fwd_sem.at[j, h], partner(0))

    def relay(i):
        h = mine(i)
        return remote(sib.at[RELAYED, h], RELAYED, h, relay_sem.at[h], partner(1))

    def arrival(j, h):
        return remote(sib.at[j, h], j, h, send_sem.at[j, h], partner(0))

    def scale(level, h, start, size):
        return w_head[h, level : level + 1, start : start + size]

    barrier = pltpu.get_barrier_semaphore()
    for i in range(half):
        for h in (other(i), mine(i)):
            fetch(1, h).start()
            fetch(2, h).start()
        if i == 0:
            for j in range(depth):
                if j == RELAYED:
                    @pl.when(inner == 1)
                    def _():
                        pl.semaphore_signal(
                            barrier, inc=1, device_id=partner(j), device_id_type=MESH
                        )
                else:
                    pl.semaphore_signal(barrier, inc=1, device_id=partner(j), device_id_type=MESH)
    fetch_w().start()
    for i in range(half):
        for h in (mine(i), other(i)):
            fetch(0, h).start()

    def block_sum(h):
        fetch(1, h).wait()
        fetch(2, h).wait()
        vt = v_buf[h].T
        vt_buf[h] = vt
        sums = [
            dot_nn(vt[:, b * SUB : (b + 1) * SUB], k_buf[h, b * SUB : (b + 1) * SUB, :])
            for b in range(count)
        ]
        slot = 0
        while len(sums) > 1:
            for b in range(0, len(sums), 2):
                sub_buf[h, slot] = sums[b].astype(jnp.bfloat16)
                slot += 1
            sums = [sums[b] + sums[b + 1] for b in range(0, len(sums), 2)]
        state[h] = sums[0].astype(jnp.bfloat16)

    def first_sends(i):
        first_send(other(i)).start()

        @pl.when(core == 0)
        def _():
            first_send(mine(i)).start()

    def local(h):
        fetch(0, h).wait()
        s = lax.broadcasted_iota(jnp.int32, (SUB, SUB), 0)
        t = lax.broadcasted_iota(jnp.int32, (SUB, SUB), 1)
        causal = s <= t
        crossing = jnp.logical_and(s < STRETCH, t >= STRETCH)
        for b in range(count):
            lo = b * SUB
            q = q_buf[h, lo : lo + SUB, :]
            scores = dot_nt(k_buf[h, lo : lo + SUB, :], q)
            weight = jnp.where(
                crossing, scale(1, h, lo, SUB), scale(0, h, lo, SUB)
            )
            weighted = jnp.where(causal, scores * weight, 0.0).astype(jnp.bfloat16)
            total = dot_nn(vt_buf[h, :, lo : lo + SUB], weighted)
            slot = 0
            for level in range(2, local_bits + 1):
                place = b >> (level - 2)
                if place % 2 == 1:
                    total += scale(level, h, lo, SUB) * dot_nt(sub_buf[h, slot + place // 2], q)
                slot += count >> (level - 1)
            out_t[h, :, lo : lo + SUB] = total

    def cross(j, h):
        level = 1 + local_bits + j
        out_t[h] += scale(level, h, 0, rows) * dot_nt(sib[j, h], q_buf[h])

    def finish(h):
        out_buf[h] = out_t[h].astype(jnp.bfloat16).T
        put(h).start()

    def guarded(condition, action):
        if condition is None:
            action()
        else:
            pl.when(condition)(action)

    def sends(j):
        if j == RELAYED:
            return inner == 1
        return bit(j) == 0 if j == last else None

    def receive(j, i):
        h = mine(i)
        guarded(bit(j) == 1 if j == last else None, lambda: arrival(j, h).wait_recv())
        if j == RELAYED:
            guarded(inner == 1, lambda: relay(i).start())
        if j >= 1:
            guarded(bit(j) == 1, lambda: forward(j, i).start())
        if j < last:
            held = state[h].astype(jnp.float32) if j == 0 else acc[i]
            total = held + sib[j, h].astype(jnp.float32)
            rounded = total.astype(jnp.bfloat16)
            run[j + 1, i] = rounded
            acc[i] = rounded.astype(jnp.float32) if j + 1 == ctx_bits else total
            guarded(sends(j + 1), lambda: stage_send(j + 1, i).start())

    block_sum(other(0))
    block_sum(mine(0))
    pl.semaphore_wait(barrier, depth - 1 + inner)
    first_sends(0)

    def open_pair(i, carry):
        block_sum(other(i))
        block_sum(mine(i))
        first_sends(i)
        receive(0, i - 1)
        return carry

    lax.fori_loop(1, half, open_pair, 0)
    receive(0, half - 1)
    fetch_w().wait()
    for level in range(1 + local_bits + depth):
        for h in range(heads):
            w_head[h, level : level + 1, :] = w_buf[level, h : h + 1, :] * level_factor(level)

    lag = [0, 1] + [half + 2 * j for j in range(depth - 2)]

    def wave(w, carry):
        for j in range(1, depth):
            i = w - lag[j]

            @pl.when(jnp.logical_and(i >= 0, i < half))
            def _():
                receive(j, i)

        @pl.when(w < half)
        def _():
            local(mine(w))
            local(other(w))

        for j in range(depth):
            i = w - lag[j]
            held = bit(j) == 1

            @pl.when(jnp.logical_and(jnp.logical_and(i >= 0, i < half), held))
            def _():
                cross(j, mine(i))

            @pl.when(jnp.logical_and(jnp.logical_and(i >= 1, i < half + 1), held))
            def _():
                h = other(i - 1)
                arrival(j, h).wait_recv()
                cross(j, h)

        final = w - lag[last]

        @pl.when(jnp.logical_and(final >= 0, final < half))
        def _():
            finish(mine(final))

        @pl.when(final >= 1)
        def _():
            finish(other(final - 1))

        return carry

    lax.fori_loop(0, lag[last] + half + 1, wave, 0)

    def close(i, carry):
        first_send(other(i)).wait_send()
        guarded(core == 0, lambda: first_send(mine(i)).wait_send())
        for h in (mine(i), other(i)):
            put(h).wait()
        for j in range(1, depth):
            guarded(sends(j), lambda: stage_send(j, i).wait_send())
            guarded(bit(j) == 1, lambda: forward(j, i).wait_send())
            if j == RELAYED:
                guarded(inner == 1, lambda: relay(i).wait_send())
        return carry

    lax.fori_loop(0, half, close, 0)


def on_device(ctx_count, grp_count, queries, keys, values, level_weights):
    rows = queries.shape[0]
    heads = level_weights.shape[1]
    count = rows // SUB
    ctx_bits = ctx_count.bit_length() - 1
    grp_bits = grp_count.bit_length() - 1
    depth = ctx_bits + grp_bits
    half = heads // 2
    bf16, f32 = jnp.bfloat16, jnp.float32
    any_spec = pl.BlockSpec(memory_space=pl.ANY)
    return pl.pallas_call(
        functools.partial(kernel, ctx_bits, grp_bits),
        out_shape=jax.ShapeDtypeStruct(queries.shape, bf16),
        in_specs=[pl.BlockSpec(memory_space=pltpu.HBM)] * 4,
        out_specs=any_spec,
        scratch_shapes=[
            pltpu.VMEM((heads, rows, DK), bf16),
            pltpu.VMEM((heads, rows, DK), bf16),
            pltpu.VMEM((heads, rows, DK), bf16),
            pltpu.VMEM(level_weights.shape, f32),
            pltpu.VMEM((heads, level_weights.shape[0], rows), f32),
            pltpu.VMEM((heads, DK, rows), bf16),
            pltpu.VMEM((heads, count - 1, DK, DK), bf16),
            pltpu.VMEM((heads, DK, DK), bf16),
            pltpu.VMEM((depth, heads, DK, DK), bf16),
            pltpu.VMEM((depth, half, DK, DK), bf16),
            pltpu.VMEM((half, DK, DK), f32),
            pltpu.VMEM((heads, DK, rows), f32),
            pltpu.VMEM((heads, rows, DK), bf16),
            pltpu.SemaphoreType.DMA((3, heads)),
            pltpu.SemaphoreType.DMA,
            pltpu.SemaphoreType.DMA((heads,)),
            pltpu.SemaphoreType.DMA((depth, heads)),
            pltpu.SemaphoreType.DMA((depth, heads)),
            pltpu.SemaphoreType.DMA((heads,)),
            pltpu.SemaphoreType.DMA((depth, heads)),
        ],
        compiler_params=pltpu.CompilerParams(
            collective_id=0, has_side_effects=True, vmem_limit_bytes=60 * 2**20
        ),
        cost_estimate=pl.CostEstimate(
            flops=2 * rows * heads * DK * DK * (9 + depth), bytes_accessed=8 * rows * heads * DK,
            transcendentals=0,
        ),
    )(queries, keys, values, level_weights)


def solution(mesh):
    return jax.shard_map(
        functools.partial(on_device, mesh.shape["ctx"], mesh.shape["grp"]),
        mesh=mesh,
        in_specs=(
            P(("grp", "ctx"), None),
            P(("grp", "ctx"), None),
            P(("grp", "ctx"), None),
            P(None, None, ("grp", "ctx")),
        ),
        out_specs=P(("grp", "ctx"), None),
        check_vma=False,
    )
```

```python
import functools
import math

import jax
import jax.numpy as jnp
from jax import lax
from jax.experimental import pallas as pl
from jax.experimental.pallas import tpu as pltpu
from jax.sharding import PartitionSpec as P

DK = 128
STRETCH = 64
SUB = 2 * STRETCH
RELAYED = 2
MESH = pl.DeviceIdType.MESH


def level_factor(level_num):
    token_count = STRETCH if level_num == 0 else STRETCH * 2 ** (level_num - 1)
    return 1.0 / math.sqrt(DK * token_count)


def dot_nt(a, b):
    return lax.dot_general(a, b, (((1,), (1,)), ((), ())), preferred_element_type=jnp.float32)


def dot_nn(a, b):
    return lax.dot_general(a, b, (((1,), (0,)), ((), ())), preferred_element_type=jnp.float32)


def kernel(
    ctx_bits, grp_bits,
    q_hbm, k_hbm, v_hbm, w_hbm, out_hbm,
    q_buf, k_buf, v_buf, w_buf, w_head, vt_buf, qt_buf, sub_buf, state, sib, run, acc, out_t, out_buf,
    in_sem, w_sem, out_sem, send_sem, fwd_sem, relay_sem, recv_sem,
):
    heads, rows = q_buf.shape[0], q_buf.shape[1]
    half = heads // 2
    count = rows // SUB
    local_bits = (rows // STRETCH).bit_length() - 1
    depth = ctx_bits + grp_bits
    last = depth - 1
    grp = lax.axis_index("grp")
    ctx = lax.axis_index("ctx")
    core = ctx % 2

    def bit(j):
        if j < ctx_bits:
            return (ctx // 2**j) % 2
        return (grp // 2 ** (j - ctx_bits)) % 2

    inner = (bit(1) + bit(2)) % 2

    def partner(j):
        step = 1 - 2 * bit(j)
        if j == RELAYED:
            return (grp, ctx + step * 2)
        if j < ctx_bits:
            return (grp, ctx + step * 2**j)
        return (grp + step * 2 ** (j - ctx_bits), ctx)

    def mine(i):
        return core * half + i

    def other(i):
        return (1 - core) * half + i

    def columns(h):
        return pl.ds(pl.multiple_of(h * DK, DK), DK)

    def fetch(n, h):
        src, dst = ((q_hbm, q_buf), (k_hbm, k_buf), (v_hbm, v_buf))[n]
        return pltpu.make_async_copy(src.at[:, columns(h)], dst.at[h], in_sem.at[n, h])

    def fetch_w():
        return pltpu.make_async_copy(w_hbm, w_buf, w_sem)

    def put(h):
        return pltpu.make_async_copy(out_buf.at[h], out_hbm.at[h], out_sem.at[h])

    def remote(src, j, h, sem, target):
        return pltpu.make_async_remote_copy(
            src_ref=src, dst_ref=sib.at[j, h], send_sem=sem, recv_sem=recv_sem.at[j, h],
            device_id=target, device_id_type=MESH,
        )

    def first_send(h):
        return remote(state.at[h], 0, h, send_sem.at[0, h], partner(0))

    def stage_send(j, i):
        return remote(run.at[j, i], j, mine(i), send_sem.at[j, mine(i)], partner(j))

    def forward(j, i):
        h = mine(i)
        return remote(sib.at[j, h], j, h, fwd_sem.at[j, h], partner(0))

    def relay(i):
        h = mine(i)
        return remote(sib.at[RELAYED, h], RELAYED, h, relay_sem.at[h], partner(1))

    def arrival(j, h):
        return remote(sib.at[j, h], j, h, send_sem.at[j, h], partner(0))

    def scale(level, h, start, size):
        return w_head[h, level : level + 1, start : start + size]

    barrier = pltpu.get_barrier_semaphore()
    for i in range(half):
        for h in (other(i), mine(i)):
            fetch(1, h).start()
            fetch(2, h).start()
        if i == 0:
            for j in range(depth):
                if j == RELAYED:
                    @pl.when(inner == 1)
                    def _():
                        pl.semaphore_signal(
                            barrier, inc=1, device_id=partner(j), device_id_type=MESH
                        )
                else:
                    pl.semaphore_signal(barrier, inc=1, device_id=partner(j), device_id_type=MESH)
    fetch_w().start()
    for i in range(half):
        for h in (mine(i), other(i)):
            fetch(0, h).start()

    def block_sum(h):
        fetch(1, h).wait()
        fetch(2, h).wait()
        vt = v_buf[h].T
        vt_buf[h] = vt
        sums = [
            dot_nn(vt[:, b * SUB : (b + 1) * SUB], k_buf[h, b * SUB : (b + 1) * SUB, :])
            for b in range(count)
        ]
        slot = 0
        while len(sums) > 1:
            for b in range(0, len(sums), 2):
                sub_buf[h, slot] = sums[b].astype(jnp.bfloat16)
                slot += 1
            sums = [sums[b] + sums[b + 1] for b in range(0, len(sums), 2)]
        state[h] = sums[0].astype(jnp.bfloat16)

    def first_sends(i):
        first_send(other(i)).start()

        @pl.when(core == 0)
        def _():
            first_send(mine(i)).start()

    def scaled(level, h, qt, lo, size):
        return (scale(level, h, lo, size) * qt).astype(jnp.bfloat16)

    def sibling(j, h):
        return jnp.where(bit(j) == 1, sib[j, h], jnp.zeros((DK, DK), jnp.bfloat16))

    def local(h):
        fetch(0, h).wait()
        qt_all = q_buf[h].T
        qt_buf[h] = qt_all
        s = lax.broadcasted_iota(jnp.int32, (SUB, SUB), 0)
        t = lax.broadcasted_iota(jnp.int32, (SUB, SUB), 1)
        causal = s <= t
        crossing = jnp.logical_and(s < STRETCH, t >= STRETCH)
        neighbour = sibling(0, h)
        for b in range(count):
            lo = b * SUB
            qt = qt_all[:, lo : lo + SUB]
            scores = dot_nn(k_buf[h, lo : lo + SUB, :], qt)
            weight = jnp.where(
                crossing, scale(1, h, lo, SUB), scale(0, h, lo, SUB)
            )
            weighted = jnp.where(causal, scores * weight, 0.0).astype(jnp.bfloat16)
            wide = qt.astype(jnp.float32)
            left = [vt_buf[h, :, lo : lo + SUB], neighbour]
            right = [weighted, scaled(1 + local_bits, h, wide, lo, SUB)]
            slot = 0
            for level in range(2, local_bits + 1):
                place = b >> (level - 2)
                if place % 2 == 1:
                    left.append(sub_buf[h, slot + place // 2])
                    right.append(scaled(level, h, wide, lo, SUB))
                slot += count >> (level - 1)
            out_t[h, :, lo : lo + SUB] = dot_nn(
                jnp.concatenate(left, axis=1), jnp.concatenate(right, axis=0)
            )

    def cross(group, h):
        wide = qt_buf[h].astype(jnp.float32)
        left = [sibling(j, h) for j in group]
        right = [scaled(1 + local_bits + j, h, wide, 0, rows) for j in group]
        return out_t[h] + dot_nn(jnp.concatenate(left, axis=1), jnp.concatenate(right, axis=0))

    def await_other(group, h):
        for j in group:
            guarded(bit(j) == 1, lambda: arrival(j, h).wait_recv())

    def middle(h):
        out_t[h] = cross(range(1, ctx_bits), h)

    def finish(h):
        out_buf[h] = cross(range(ctx_bits, depth), h).astype(jnp.bfloat16)
        put(h).start()

    def guarded(condition, action):
        if condition is None:
            action()
        else:
            pl.when(condition)(action)

    def sends(j):
        if j == RELAYED:
            return inner == 1
        return bit(j) == 0 if j == last else None

    def receive(j, i):
        h = mine(i)
        guarded(bit(j) == 1 if j == last else None, lambda: arrival(j, h).wait_recv())
        if j == RELAYED:
            guarded(inner == 1, lambda: relay(i).start())
        if j >= 1:
            guarded(bit(j) == 1, lambda: forward(j, i).start())
        if j < last:
            held = state[h].astype(jnp.float32) if j == 0 else acc[i]
            total = held + sib[j, h].astype(jnp.float32)
            rounded = total.astype(jnp.bfloat16)
            run[j + 1, i] = rounded
            acc[i] = rounded.astype(jnp.float32) if j + 1 == ctx_bits else total
            guarded(sends(j + 1), lambda: stage_send(j + 1, i).start())

    block_sum(other(0))
    block_sum(mine(0))
    pl.semaphore_wait(barrier, depth - 1 + inner)
    first_sends(0)

    def open_pair(i, carry):
        block_sum(other(i))
        block_sum(mine(i))
        first_sends(i)
        receive(0, i - 1)
        return carry

    lax.fori_loop(1, half, open_pair, 0)
    receive(0, half - 1)
    fetch_w().wait()
    for level in range(1 + local_bits + depth):
        for h in range(heads):
            w_head[h, level : level + 1, :] = w_buf[level, h : h + 1, :] * level_factor(level)

    lag = [0, 1, half] + [2 * half + 2 * j for j in range(depth - 3)]
    lag_middle = max(2 * half, lag[ctx_bits - 1] + 1)

    def between(i, low, high):
        return jnp.logical_and(i >= low, i < high)

    def wave(w, carry):
        for j in range(1, depth):
            i = w - lag[j]
            guarded(between(i, 0, half), functools.partial(receive, j, i))

        @pl.when(w < heads)
        def _():
            h = ((core + w) % 2) * half + w // 2

            @pl.when(jnp.logical_and(w % 2 == 1, bit(0) == 1))
            def _():
                arrival(0, h).wait_recv()

            local(h)

        i_middle = w - lag_middle

        @pl.when(between(i_middle, 0, half))
        def _():
            middle(mine(i_middle))
            await_other(range(1, ctx_bits), other(i_middle))
            middle(other(i_middle))

        final = w - lag[last]

        @pl.when(between(final, 0, half))
        def _():
            finish(mine(final))

        @pl.when(final >= 1)
        def _():
            await_other(range(ctx_bits, depth), other(final - 1))
            finish(other(final - 1))

        return carry

    lax.fori_loop(0, lag[last] + half + 1, wave, 0)

    def close(i, carry):
        first_send(other(i)).wait_send()
        guarded(core == 0, lambda: first_send(mine(i)).wait_send())
        for h in (mine(i), other(i)):
            put(h).wait()
        for j in range(1, depth):
            guarded(sends(j), lambda: stage_send(j, i).wait_send())
            guarded(bit(j) == 1, lambda: forward(j, i).wait_send())
            if j == RELAYED:
                guarded(inner == 1, lambda: relay(i).wait_send())
        return carry

    lax.fori_loop(0, half, close, 0)


def on_device(ctx_count, grp_count, queries, keys, values, level_weights):
    rows = queries.shape[0]
    heads = level_weights.shape[1]
    count = rows // SUB
    ctx_bits = ctx_count.bit_length() - 1
    grp_bits = grp_count.bit_length() - 1
    depth = ctx_bits + grp_bits
    half = heads // 2
    bf16, f32 = jnp.bfloat16, jnp.float32
    any_spec = pl.BlockSpec(memory_space=pl.ANY)
    out = pl.pallas_call(
        functools.partial(kernel, ctx_bits, grp_bits),
        out_shape=jax.ShapeDtypeStruct((heads, DK, rows), bf16),
        in_specs=[pl.BlockSpec(memory_space=pltpu.HBM)] * 4,
        out_specs=any_spec,
        scratch_shapes=[
            pltpu.VMEM((heads, rows, DK), bf16),
            pltpu.VMEM((heads, rows, DK), bf16),
            pltpu.VMEM((heads, rows, DK), bf16),
            pltpu.VMEM(level_weights.shape, f32),
            pltpu.VMEM((heads, level_weights.shape[0], rows), f32),
            pltpu.VMEM((heads, DK, rows), bf16),
            pltpu.VMEM((heads, DK, rows), bf16),
            pltpu.VMEM((heads, count - 1, DK, DK), bf16),
            pltpu.VMEM((heads, DK, DK), bf16),
            pltpu.VMEM((depth, heads, DK, DK), bf16),
            pltpu.VMEM((depth, half, DK, DK), bf16),
            pltpu.VMEM((half, DK, DK), f32),
            pltpu.VMEM((heads, DK, rows), f32),
            pltpu.VMEM((heads, DK, rows), bf16),
            pltpu.SemaphoreType.DMA((3, heads)),
            pltpu.SemaphoreType.DMA,
            pltpu.SemaphoreType.DMA((heads,)),
            pltpu.SemaphoreType.DMA((depth, heads)),
            pltpu.SemaphoreType.DMA((depth, heads)),
            pltpu.SemaphoreType.DMA((heads,)),
            pltpu.SemaphoreType.DMA((depth, heads)),
        ],
        compiler_params=pltpu.CompilerParams(
            collective_id=0, has_side_effects=True, vmem_limit_bytes=60 * 2**20
        ),
        cost_estimate=pl.CostEstimate(
            flops=2 * rows * heads * DK * DK * (9 + depth), bytes_accessed=8 * rows * heads * DK,
            transcendentals=0,
        ),
    )(queries, keys, values, level_weights)
    return out.transpose(2, 0, 1).reshape(rows, heads * DK)


def solution(mesh):
    return jax.shard_map(
        functools.partial(on_device, mesh.shape["ctx"], mesh.shape["grp"]),
        mesh=mesh,
        in_specs=(
            P(("grp", "ctx"), None),
            P(("grp", "ctx"), None),
            P(("grp", "ctx"), None),
            P(None, None, ("grp", "ctx")),
        ),
        out_specs=P(("grp", "ctx"), None),
        check_vma=False,
    )
```

```python
import functools
import math

import jax
import jax.numpy as jnp
from jax import lax
from jax.experimental import pallas as pl
from jax.experimental.pallas import tpu as pltpu
from jax.sharding import PartitionSpec as P

DK = 128
STRETCH = 64
SUB = 2 * STRETCH
RELAYED = 2
MESH = pl.DeviceIdType.MESH


def level_factor(level_num):
    token_count = STRETCH if level_num == 0 else STRETCH * 2 ** (level_num - 1)
    return 1.0 / math.sqrt(DK * token_count)


def dot_nt(a, b):
    return lax.dot_general(a, b, (((1,), (1,)), ((), ())), preferred_element_type=jnp.float32)


def dot_nn(a, b):
    return lax.dot_general(a, b, (((1,), (0,)), ((), ())), preferred_element_type=jnp.float32)


def kernel(
    ctx_bits, grp_bits,
    q_hbm, k_hbm, v_hbm, w_hbm, out_hbm,
    q_buf, k_buf, v_buf, w_buf, w_head, vt_buf, qt_buf, sub_buf, state, sib, run, acc, out_t, out_buf,
    in_sem, w_sem, out_sem, send_sem, fwd_sem, relay_sem, recv_sem,
):
    heads, rows = q_buf.shape[0], q_buf.shape[1]
    half = heads // 2
    count = rows // SUB
    local_bits = (rows // STRETCH).bit_length() - 1
    depth = ctx_bits + grp_bits
    last = depth - 1
    grp = lax.axis_index("grp")
    ctx = lax.axis_index("ctx")
    core = ctx % 2

    def bit(j):
        if j < ctx_bits:
            return (ctx // 2**j) % 2
        return (grp // 2 ** (j - ctx_bits)) % 2

    inner = (bit(1) + bit(2)) % 2

    def partner(j):
        step = 1 - 2 * bit(j)
        if j == RELAYED:
            return (grp, ctx + step * 2)
        if j < ctx_bits:
            return (grp, ctx + step * 2**j)
        return (grp + step * 2 ** (j - ctx_bits), ctx)

    def mine(i):
        return core * half + i

    def other(i):
        return (1 - core) * half + i

    def columns(h):
        return pl.ds(pl.multiple_of(h * DK, DK), DK)

    def fetch(n, h):
        src, dst = ((q_hbm, q_buf), (k_hbm, k_buf), (v_hbm, v_buf))[n]
        return pltpu.make_async_copy(src.at[:, columns(h)], dst.at[h], in_sem.at[n, h])

    def fetch_w():
        return pltpu.make_async_copy(w_hbm, w_buf, w_sem)

    def put(h):
        return pltpu.make_async_copy(out_buf.at[h], out_hbm.at[:, columns(h)], out_sem.at[h])

    def remote(src, j, h, sem, target):
        return pltpu.make_async_remote_copy(
            src_ref=src, dst_ref=sib.at[j, h], send_sem=sem, recv_sem=recv_sem.at[j, h],
            device_id=target, device_id_type=MESH,
        )

    def first_send(h):
        return remote(state.at[h], 0, h, send_sem.at[0, h], partner(0))

    def stage_send(j, i):
        return remote(run.at[j, i], j, mine(i), send_sem.at[j, mine(i)], partner(j))

    def forward(j, i):
        h = mine(i)
        return remote(sib.at[j, h], j, h, fwd_sem.at[j, h], partner(0))

    def relay(i):
        h = mine(i)
        return remote(sib.at[RELAYED, h], RELAYED, h, relay_sem.at[h], partner(1))

    def arrival(j, h):
        return remote(sib.at[j, h], j, h, send_sem.at[j, h], partner(0))

    def scale(level, h, start, size):
        return w_head[h, level : level + 1, start : start + size]

    barrier = pltpu.get_barrier_semaphore()
    for i in range(half):
        for h in (other(i), mine(i)):
            fetch(1, h).start()
            fetch(2, h).start()
        if i == 0:
            for j in range(depth):
                if j == RELAYED:
                    @pl.when(inner == 1)
                    def _():
                        pl.semaphore_signal(
                            barrier, inc=1, device_id=partner(j), device_id_type=MESH
                        )
                else:
                    pl.semaphore_signal(barrier, inc=1, device_id=partner(j), device_id_type=MESH)
    fetch_w().start()
    for i in range(half):
        for h in (mine(i), other(i)):
            fetch(0, h).start()

    def block_sum(h):
        fetch(1, h).wait()
        fetch(2, h).wait()
        vt = v_buf[h].T
        vt_buf[h] = vt
        sums = [
            dot_nn(vt[:, b * SUB : (b + 1) * SUB], k_buf[h, b * SUB : (b + 1) * SUB, :])
            for b in range(count)
        ]
        slot = 0
        while len(sums) > 1:
            for b in range(0, len(sums), 2):
                sub_buf[h, slot] = sums[b].astype(jnp.bfloat16)
                slot += 1
            sums = [sums[b] + sums[b + 1] for b in range(0, len(sums), 2)]
        state[h] = sums[0].astype(jnp.bfloat16)

    def first_sends(i):
        first_send(other(i)).start()

        @pl.when(core == 0)
        def _():
            first_send(mine(i)).start()

    def scaled(level, h, qt, lo, size):
        return (scale(level, h, lo, size) * qt).astype(jnp.bfloat16)

    def sibling(j, h):
        return jnp.where(bit(j) == 1, sib[j, h], jnp.zeros((DK, DK), jnp.bfloat16))

    def local(h):
        fetch(0, h).wait()
        qt_all = q_buf[h].T
        qt_buf[h] = qt_all
        s = lax.broadcasted_iota(jnp.int32, (SUB, SUB), 0)
        t = lax.broadcasted_iota(jnp.int32, (SUB, SUB), 1)
        causal = s <= t
        crossing = jnp.logical_and(s < STRETCH, t >= STRETCH)
        neighbour = sibling(0, h)
        for b in range(count):
            lo = b * SUB
            qt = qt_all[:, lo : lo + SUB]
            scores = dot_nn(k_buf[h, lo : lo + SUB, :], qt)
            weight = jnp.where(
                crossing, scale(1, h, lo, SUB), scale(0, h, lo, SUB)
            )
            weighted = jnp.where(causal, scores * weight, 0.0).astype(jnp.bfloat16)
            wide = qt.astype(jnp.float32)
            left = [vt_buf[h, :, lo : lo + SUB], neighbour]
            right = [weighted, scaled(1 + local_bits, h, wide, lo, SUB)]
            slot = 0
            for level in range(2, local_bits + 1):
                place = b >> (level - 2)
                if place % 2 == 1:
                    left.append(sub_buf[h, slot + place // 2])
                    right.append(scaled(level, h, wide, lo, SUB))
                slot += count >> (level - 1)
            out_t[h, :, lo : lo + SUB] = dot_nn(
                jnp.concatenate(left, axis=1), jnp.concatenate(right, axis=0)
            )

    def cross(group, h):
        wide = qt_buf[h].astype(jnp.float32)
        left = [sibling(j, h) for j in group]
        right = [scaled(1 + local_bits + j, h, wide, 0, rows) for j in group]
        return out_t[h] + dot_nn(jnp.concatenate(left, axis=1), jnp.concatenate(right, axis=0))

    def await_other(group, h):
        for j in group:
            guarded(bit(j) == 1, lambda: arrival(j, h).wait_recv())

    def middle(h):
        out_t[h] = cross(range(1, ctx_bits), h)

    def finish(h):
        out_buf[h] = cross(range(ctx_bits, depth), h).T
        put(h).start()

    def guarded(condition, action):
        if condition is None:
            action()
        else:
            pl.when(condition)(action)

    def sends(j):
        if j == RELAYED:
            return inner == 1
        return bit(j) == 0 if j == last else None

    def receive(j, i):
        h = mine(i)
        guarded(bit(j) == 1 if j == last else None, lambda: arrival(j, h).wait_recv())
        if j == RELAYED:
            guarded(inner == 1, lambda: relay(i).start())
        if j >= 1:
            guarded(bit(j) == 1, lambda: forward(j, i).start())
        if j < last:
            held = state[h].astype(jnp.float32) if j == 0 else acc[i]
            total = held + sib[j, h].astype(jnp.float32)
            rounded = total.astype(jnp.bfloat16)
            run[j + 1, i] = rounded
            acc[i] = rounded.astype(jnp.float32) if j + 1 == ctx_bits else total
            guarded(sends(j + 1), lambda: stage_send(j + 1, i).start())

    block_sum(other(0))
    block_sum(mine(0))
    pl.semaphore_wait(barrier, depth - 1 + inner)
    first_sends(0)

    def open_pair(i, carry):
        block_sum(other(i))
        block_sum(mine(i))
        first_sends(i)
        receive(0, i - 1)
        return carry

    lax.fori_loop(1, half, open_pair, 0)
    fetch_w().wait()
    for level in range(1 + local_bits + depth):
        for h in range(heads):
            w_head[h, level : level + 1, :] = w_buf[level, h : h + 1, :] * level_factor(level)

    receive(0, half - 1)

    lag = [0] + [1 + 2 * j for j in range(depth - 1)]
    lag_middle = max(half + 2, lag[ctx_bits - 1] + 1)

    def between(i, low, high):
        return jnp.logical_and(i >= low, i < high)

    def wave(w, carry):
        for j in range(1, depth):
            i = w - lag[j]
            guarded(between(i, 0, half), functools.partial(receive, j, i))

        @pl.when(w < heads)
        def _():
            h = ((core + w) % 2) * half + w // 2

            @pl.when(jnp.logical_and(w % 2 == 1, bit(0) == 1))
            def _():
                arrival(0, h).wait_recv()

            local(h)

        i_middle = w - lag_middle

        @pl.when(between(i_middle, 0, half))
        def _():
            middle(mine(i_middle))
            await_other(range(1, ctx_bits), other(i_middle))
            middle(other(i_middle))

        final = w - lag[last]

        @pl.when(between(final, 0, half))
        def _():
            finish(mine(final))

        @pl.when(final >= 1)
        def _():
            await_other(range(ctx_bits, depth), other(final - 1))
            finish(other(final - 1))

        return carry

    lax.fori_loop(0, lag[last] + half + 1, wave, 0)

    def close(i, carry):
        first_send(other(i)).wait_send()
        guarded(core == 0, lambda: first_send(mine(i)).wait_send())
        for h in (mine(i), other(i)):
            put(h).wait()
        for j in range(1, depth):
            guarded(sends(j), lambda: stage_send(j, i).wait_send())
            guarded(bit(j) == 1, lambda: forward(j, i).wait_send())
            if j == RELAYED:
                guarded(inner == 1, lambda: relay(i).wait_send())
        return carry

    lax.fori_loop(0, half, close, 0)


def on_device(ctx_count, grp_count, queries, keys, values, level_weights):
    rows = queries.shape[0]
    heads = level_weights.shape[1]
    count = rows // SUB
    ctx_bits = ctx_count.bit_length() - 1
    grp_bits = grp_count.bit_length() - 1
    depth = ctx_bits + grp_bits
    half = heads // 2
    bf16, f32 = jnp.bfloat16, jnp.float32
    any_spec = pl.BlockSpec(memory_space=pl.ANY)
    out = pl.pallas_call(
        functools.partial(kernel, ctx_bits, grp_bits),
        out_shape=jax.ShapeDtypeStruct(queries.shape, f32),
        in_specs=[pl.BlockSpec(memory_space=pltpu.HBM)] * 4,
        out_specs=any_spec,
        scratch_shapes=[
            pltpu.VMEM((heads, rows, DK), bf16),
            pltpu.VMEM((heads, rows, DK), bf16),
            pltpu.VMEM((heads, rows, DK), bf16),
            pltpu.VMEM(level_weights.shape, f32),
            pltpu.VMEM((heads, level_weights.shape[0], rows), f32),
            pltpu.VMEM((heads, DK, rows), bf16),
            pltpu.VMEM((heads, DK, rows), bf16),
            pltpu.VMEM((heads, count - 1, DK, DK), bf16),
            pltpu.VMEM((heads, DK, DK), bf16),
            pltpu.VMEM((depth, heads, DK, DK), bf16),
            pltpu.VMEM((depth, half, DK, DK), bf16),
            pltpu.VMEM((half, DK, DK), f32),
            pltpu.VMEM((heads, DK, rows), f32),
            pltpu.VMEM((heads, rows, DK), f32),
            pltpu.SemaphoreType.DMA((3, heads)),
            pltpu.SemaphoreType.DMA,
            pltpu.SemaphoreType.DMA((heads,)),
            pltpu.SemaphoreType.DMA((depth, heads)),
            pltpu.SemaphoreType.DMA((depth, heads)),
            pltpu.SemaphoreType.DMA((heads,)),
            pltpu.SemaphoreType.DMA((depth, heads)),
        ],
        compiler_params=pltpu.CompilerParams(
            collective_id=0, has_side_effects=True, vmem_limit_bytes=60 * 2**20
        ),
        cost_estimate=pl.CostEstimate(
            flops=2 * rows * heads * DK * DK * (9 + depth), bytes_accessed=8 * rows * heads * DK,
            transcendentals=0,
        ),
    )(queries, keys, values, level_weights)
    return out.astype(bf16)


def solution(mesh):
    return jax.shard_map(
        functools.partial(on_device, mesh.shape["ctx"], mesh.shape["grp"]),
        mesh=mesh,
        in_specs=(
            P(("grp", "ctx"), None),
            P(("grp", "ctx"), None),
            P(("grp", "ctx"), None),
            P(None, None, ("grp", "ctx")),
        ),
        out_specs=P(("grp", "ctx"), None),
        check_vma=False,
    )
```

```python
import functools
import math

import jax
import jax.numpy as jnp
from jax import lax
from jax.experimental import pallas as pl
from jax.experimental.pallas import tpu as pltpu
from jax.sharding import PartitionSpec as P

DK = 128
STRETCH = 64
SUB = 2 * STRETCH
RELAYED = 2
MESH = pl.DeviceIdType.MESH


def level_factor(level_num):
    token_count = STRETCH if level_num == 0 else STRETCH * 2 ** (level_num - 1)
    return 1.0 / math.sqrt(DK * token_count)


def dot_nt(a, b):
    return lax.dot_general(a, b, (((1,), (1,)), ((), ())), preferred_element_type=jnp.float32)


def dot_nn(a, b):
    return lax.dot_general(a, b, (((1,), (0,)), ((), ())), preferred_element_type=jnp.float32)


def kernel(
    ctx_bits, grp_bits,
    q_hbm, k_hbm, v_hbm, w_hbm, out_hbm,
    q_buf, k_buf, v_buf, w_buf, w_head, vt_buf, qt_buf, sub_buf, state, sib, run, acc, out_t, out_buf,
    in_sem, w_sem, out_sem, send_sem, fwd_sem, relay_sem, recv_sem,
):
    heads, rows = q_buf.shape[0], q_buf.shape[1]
    half = heads // 2
    count = rows // SUB
    local_bits = (rows // STRETCH).bit_length() - 1
    depth = ctx_bits + grp_bits
    last = depth - 1
    grp = lax.axis_index("grp")
    ctx = lax.axis_index("ctx")
    core = ctx % 2

    def bit(j):
        if j < ctx_bits:
            return (ctx // 2**j) % 2
        return (grp // 2 ** (j - ctx_bits)) % 2

    inner = (bit(1) + bit(2)) % 2

    def partner(j):
        step = 1 - 2 * bit(j)
        if j == RELAYED:
            return (grp, ctx + step * 2)
        if j < ctx_bits:
            return (grp, ctx + step * 2**j)
        return (grp + step * 2 ** (j - ctx_bits), ctx)

    def mine(i):
        return core * half + i

    def other(i):
        return (1 - core) * half + i

    def columns(h):
        return pl.ds(pl.multiple_of(h * DK, DK), DK)

    def fetch(n, h):
        src, dst = ((q_hbm, q_buf), (k_hbm, k_buf), (v_hbm, v_buf))[n]
        return pltpu.make_async_copy(src.at[:, columns(h)], dst.at[h], in_sem.at[n, h])

    def fetch_w():
        return pltpu.make_async_copy(w_hbm, w_buf, w_sem)

    def put(h):
        return pltpu.make_async_copy(out_buf.at[h], out_hbm.at[h], out_sem.at[h])

    def remote(src, j, h, sem, target):
        return pltpu.make_async_remote_copy(
            src_ref=src, dst_ref=sib.at[j, h], send_sem=sem, recv_sem=recv_sem.at[j, h],
            device_id=target, device_id_type=MESH,
        )

    def first_send(h):
        return remote(state.at[h], 0, h, send_sem.at[0, h], partner(0))

    def stage_send(j, i):
        return remote(run.at[j, i], j, mine(i), send_sem.at[j, mine(i)], partner(j))

    def forward(j, i):
        h = mine(i)
        return remote(sib.at[j, h], j, h, fwd_sem.at[j, h], partner(0))

    def relay(i):
        h = mine(i)
        return remote(sib.at[RELAYED, h], RELAYED, h, relay_sem.at[h], partner(1))

    def arrival(j, h):
        return remote(sib.at[j, h], j, h, send_sem.at[j, h], partner(0))

    def scale(level, h, start, size):
        return w_head[h, level : level + 1, start : start + size]

    barrier = pltpu.get_barrier_semaphore()
    for i in range(half):
        for h in (other(i), mine(i)):
            fetch(1, h).start()
            fetch(2, h).start()
        if i == 0:
            for j in range(depth):
                if j == RELAYED:
                    @pl.when(inner == 1)
                    def _():
                        pl.semaphore_signal(
                            barrier, inc=1, device_id=partner(j), device_id_type=MESH
                        )
                else:
                    pl.semaphore_signal(barrier, inc=1, device_id=partner(j), device_id_type=MESH)
    fetch_w().start()
    for i in range(half):
        for h in (mine(i), other(i)):
            fetch(0, h).start()

    def block_sums(i):
        for h in (other(i), mine(i)):
            fetch(1, h).wait()
            fetch(2, h).wait()
        for h in (other(i), mine(i)):
            block_sum(h)

    def block_sum(h):
        vt = v_buf[h].T
        vt_buf[h] = vt
        sums = [
            dot_nn(vt[:, b * SUB : (b + 1) * SUB], k_buf[h, b * SUB : (b + 1) * SUB, :])
            for b in range(count)
        ]
        slot = 0
        while len(sums) > 1:
            for b in range(0, len(sums), 2):
                sub_buf[h, slot] = sums[b].astype(jnp.bfloat16)
                slot += 1
            sums = [sums[b] + sums[b + 1] for b in range(0, len(sums), 2)]
        state[h] = sums[0].astype(jnp.bfloat16)

    def first_sends(i):
        first_send(other(i)).start()

        @pl.when(core == 0)
        def _():
            first_send(mine(i)).start()

    def scaled(level, h, qt, lo, size):
        return (scale(level, h, lo, size) * qt).astype(jnp.bfloat16)

    def sibling(j, h):
        return jnp.where(bit(j) == 1, sib[j, h], jnp.zeros((DK, DK), jnp.bfloat16))

    def local(h):
        qt_all = q_buf[h].T
        qt_buf[h] = qt_all
        s = lax.broadcasted_iota(jnp.int32, (SUB, SUB), 0)
        t = lax.broadcasted_iota(jnp.int32, (SUB, SUB), 1)
        causal = s <= t
        crossing = jnp.logical_and(s < STRETCH, t >= STRETCH)
        neighbour = sibling(0, h)
        for b in range(count):
            lo = b * SUB
            qt = qt_all[:, lo : lo + SUB]
            scores = dot_nn(k_buf[h, lo : lo + SUB, :], qt)
            weight = jnp.where(
                crossing, scale(1, h, lo, SUB), scale(0, h, lo, SUB)
            )
            weighted = jnp.where(causal, scores * weight, 0.0).astype(jnp.bfloat16)
            wide = qt.astype(jnp.float32)
            left = [vt_buf[h, :, lo : lo + SUB], neighbour]
            right = [weighted, scaled(1 + local_bits, h, wide, lo, SUB)]
            slot = 0
            for level in range(2, local_bits + 1):
                place = b >> (level - 2)
                if place % 2 == 1:
                    left.append(sub_buf[h, slot + place // 2])
                    right.append(scaled(level, h, wide, lo, SUB))
                slot += count >> (level - 1)
            out_t[h, :, lo : lo + SUB] = dot_nn(
                jnp.concatenate(left, axis=1), jnp.concatenate(right, axis=0)
            )

    def cross(group, h):
        wide = qt_buf[h].astype(jnp.float32)
        left = [sibling(j, h) for j in group]
        right = [scaled(1 + local_bits + j, h, wide, 0, rows) for j in group]
        return out_t[h] + dot_nn(jnp.concatenate(left, axis=1), jnp.concatenate(right, axis=0))

    def await_other(group, h):
        for j in group:
            guarded(bit(j) == 1, lambda: arrival(j, h).wait_recv())

    def middle(h):
        return cross(range(1, ctx_bits), h)

    def finish(h):
        return cross(range(ctx_bits, depth), h).astype(jnp.bfloat16)

    def guarded(condition, action):
        if condition is None:
            action()
        else:
            pl.when(condition)(action)

    def sends(j):
        if j == RELAYED:
            return inner == 1
        return bit(j) == 0 if j == last else None

    def receive(j, i):
        h = mine(i)
        guarded(bit(j) == 1 if j == last else None, lambda: arrival(j, h).wait_recv())
        if j == RELAYED:
            guarded(inner == 1, lambda: relay(i).start())
        if j >= 1:
            guarded(bit(j) == 1, lambda: forward(j, i).start())
        if j < last:
            held = state[h].astype(jnp.float32) if j == 0 else acc[i]
            total = held + sib[j, h].astype(jnp.float32)
            rounded = total.astype(jnp.bfloat16)
            run[j + 1, i] = rounded
            acc[i] = rounded.astype(jnp.float32) if j + 1 == ctx_bits else total
            guarded(sends(j + 1), lambda: stage_send(j + 1, i).start())

    block_sums(0)
    pl.semaphore_wait(barrier, depth - 1 + inner)
    first_sends(0)

    def open_pair(i, carry):
        block_sums(i)
        first_sends(i)
        receive(0, i - 1)
        return carry

    lax.fori_loop(1, half, open_pair, 0)
    fetch_w().wait()
    for level in range(1 + local_bits + depth):
        for h in range(heads):
            w_head[h, level : level + 1, :] = w_buf[level, h : h + 1, :] * level_factor(level)

    receive(0, half - 1)
    lag = [0] + [1 + 2 * j for j in range(depth - 1)]
    lag_middle = max(half + 1, lag[ctx_bits - 1] + 1)

    def between(i, low, high):
        return jnp.logical_and(i >= low, i < high)

    def wave(w, carry):
        for j in range(1, depth):
            i = w - lag[j]
            guarded(between(i, 0, half), functools.partial(receive, j, i))

        @pl.when(w < half)
        def _():
            await_other(range(1), other(w))
            for h in (mine(w), other(w)):
                fetch(0, h).wait()
            for h in (mine(w), other(w)):
                local(h)

        i_middle = w - lag_middle

        @pl.when(between(i_middle, 0, half))
        def _():
            await_other(range(1, ctx_bits), other(i_middle))
            first = middle(mine(i_middle))
            second = middle(other(i_middle))
            out_t[mine(i_middle)] = first
            out_t[other(i_middle)] = second

        final = w - lag[last]

        @pl.when(between(final, 1, half))
        def _():
            await_other(range(ctx_bits, depth), other(final - 1))
            first = finish(mine(final))
            second = finish(other(final - 1))
            out_buf[mine(final)] = first
            out_buf[other(final - 1)] = second
            put(mine(final)).start()
            put(other(final - 1)).start()

        @pl.when(final == 0)
        def _():
            out_buf[mine(final)] = finish(mine(final))
            put(mine(final)).start()

        @pl.when(final == half)
        def _():
            await_other(range(ctx_bits, depth), other(final - 1))
            out_buf[other(final - 1)] = finish(other(final - 1))
            put(other(final - 1)).start()

        return carry

    lax.fori_loop(0, lag[last] + half + 1, wave, 0)

    def close(i, carry):
        first_send(other(i)).wait_send()
        guarded(core == 0, lambda: first_send(mine(i)).wait_send())
        for h in (mine(i), other(i)):
            put(h).wait()
        for j in range(1, depth):
            guarded(sends(j), lambda: stage_send(j, i).wait_send())
            guarded(bit(j) == 1, lambda: forward(j, i).wait_send())
            if j == RELAYED:
                guarded(inner == 1, lambda: relay(i).wait_send())
        return carry

    lax.fori_loop(0, half, close, 0)


def on_device(ctx_count, grp_count, queries, keys, values, level_weights):
    rows = queries.shape[0]
    heads = level_weights.shape[1]
    count = rows // SUB
    ctx_bits = ctx_count.bit_length() - 1
    grp_bits = grp_count.bit_length() - 1
    depth = ctx_bits + grp_bits
    half = heads // 2
    bf16, f32 = jnp.bfloat16, jnp.float32
    any_spec = pl.BlockSpec(memory_space=pl.ANY)
    out = pl.pallas_call(
        functools.partial(kernel, ctx_bits, grp_bits),
        out_shape=jax.ShapeDtypeStruct((heads, DK, rows), bf16),
        in_specs=[pl.BlockSpec(memory_space=pltpu.HBM)] * 4,
        out_specs=any_spec,
        scratch_shapes=[
            pltpu.VMEM((heads, rows, DK), bf16),
            pltpu.VMEM((heads, rows, DK), bf16),
            pltpu.VMEM((heads, rows, DK), bf16),
            pltpu.VMEM(level_weights.shape, f32),
            pltpu.VMEM((heads, level_weights.shape[0], rows), f32),
            pltpu.VMEM((heads, DK, rows), bf16),
            pltpu.VMEM((heads, DK, rows), bf16),
            pltpu.VMEM((heads, count - 1, DK, DK), bf16),
            pltpu.VMEM((heads, DK, DK), bf16),
            pltpu.VMEM((depth, heads, DK, DK), bf16),
            pltpu.VMEM((depth, half, DK, DK), bf16),
            pltpu.VMEM((half, DK, DK), f32),
            pltpu.VMEM((heads, DK, rows), f32),
            pltpu.VMEM((heads, DK, rows), bf16),
            pltpu.SemaphoreType.DMA((3, heads)),
            pltpu.SemaphoreType.DMA,
            pltpu.SemaphoreType.DMA((heads,)),
            pltpu.SemaphoreType.DMA((depth, heads)),
            pltpu.SemaphoreType.DMA((depth, heads)),
            pltpu.SemaphoreType.DMA((heads,)),
            pltpu.SemaphoreType.DMA((depth, heads)),
        ],
        compiler_params=pltpu.CompilerParams(
            collective_id=0, has_side_effects=True, vmem_limit_bytes=60 * 2**20
        ),
        cost_estimate=pl.CostEstimate(
            flops=2 * rows * heads * DK * DK * (9 + depth), bytes_accessed=8 * rows * heads * DK,
            transcendentals=0,
        ),
    )(queries, keys, values, level_weights)
    return out.transpose(2, 0, 1).reshape(rows, heads * DK)


def solution(mesh):
    return jax.shard_map(
        functools.partial(on_device, mesh.shape["ctx"], mesh.shape["grp"]),
        mesh=mesh,
        in_specs=(
            P(("grp", "ctx"), None),
            P(("grp", "ctx"), None),
            P(("grp", "ctx"), None),
            P(None, None, ("grp", "ctx")),
        ),
        out_specs=P(("grp", "ctx"), None),
        check_vma=False,
    )
```

```python
import functools
import math

import jax
import jax.numpy as jnp
from jax import lax
from jax.experimental import pallas as pl
from jax.experimental.pallas import tpu as pltpu
from jax.sharding import PartitionSpec as P

DK = 128
STRETCH = 64
SUB = 2 * STRETCH
MESH = pl.DeviceIdType.MESH


def level_factor(level_num):
    token_count = STRETCH if level_num == 0 else STRETCH * 2 ** (level_num - 1)
    return 1.0 / math.sqrt(DK * token_count)


def dot_nt(a, b):
    return lax.dot_general(a, b, (((1,), (1,)), ((), ())), preferred_element_type=jnp.float32)


def dot_nn(a, b):
    return lax.dot_general(a, b, (((1,), (0,)), ((), ())), preferred_element_type=jnp.float32)


def kernel(
    ctx_bits, grp_bits,
    q_hbm, k_hbm, v_hbm, w_hbm, out_hbm,
    q_buf, k_buf, v_buf, w_buf, w_head, vt_buf, qt_buf, sub_buf, state, sib, run, acc, out_t, out_buf,
    in_sem, w_sem, out_sem, send_sem, fwd_sem, recv_sem,
):
    heads, rows = q_buf.shape[0], q_buf.shape[1]
    half = heads // 2
    count = rows // SUB
    local_bits = (rows // STRETCH).bit_length() - 1
    depth = ctx_bits + grp_bits
    last = depth - 1
    grp = lax.axis_index("grp")
    ctx = lax.axis_index("ctx")
    core = ctx % 2

    def bit(j):
        if j < ctx_bits:
            return (ctx // 2**j) % 2
        return (grp // 2 ** (j - ctx_bits)) % 2

    def partner(j):
        step = 1 - 2 * bit(j)
        if j < ctx_bits:
            return (grp, ctx + step * 2**j)
        return (grp + step * 2 ** (j - ctx_bits), ctx)

    def mine(i):
        return core * half + i

    def other(i):
        return (1 - core) * half + i

    def columns(h):
        return pl.ds(pl.multiple_of(h * DK, DK), DK)

    def fetch(n, h):
        src, dst = ((q_hbm, q_buf), (k_hbm, k_buf), (v_hbm, v_buf))[n]
        return pltpu.make_async_copy(src.at[:, columns(h)], dst.at[h], in_sem.at[n, h])

    def fetch_w():
        return pltpu.make_async_copy(w_hbm, w_buf, w_sem)

    def put(h):
        return pltpu.make_async_copy(out_buf.at[h], out_hbm.at[h], out_sem.at[h])

    def remote(src, j, h, sem, target):
        return pltpu.make_async_remote_copy(
            src_ref=src, dst_ref=sib.at[j, h], send_sem=sem, recv_sem=recv_sem.at[j, h],
            device_id=target, device_id_type=MESH,
        )

    def first_send(h):
        return remote(state.at[h], 0, h, send_sem.at[0, h], partner(0))

    def stage_send(j, i):
        return remote(run.at[j, i], j, mine(i), send_sem.at[j, mine(i)], partner(j))

    def forward(j, i):
        h = mine(i)
        return remote(sib.at[j, h], j, h, fwd_sem.at[j, h], partner(0))

    def arrival(j, h):
        return remote(sib.at[j, h], j, h, send_sem.at[j, h], partner(0))

    def scale(level, h, start, size):
        return w_head[h, level : level + 1, start : start + size]

    barrier = pltpu.get_barrier_semaphore()
    for i in range(half):
        for h in (other(i), mine(i)):
            fetch(1, h).start()
            fetch(2, h).start()
        if i == 0:
            for j in range(depth):
                pl.semaphore_signal(barrier, inc=1, device_id=partner(j), device_id_type=MESH)
    fetch_w().start()
    for i in range(half):
        for h in (mine(i), other(i)):
            fetch(0, h).start()

    def block_sum(h):
        fetch(1, h).wait()
        fetch(2, h).wait()
        vt = v_buf[h].T
        vt_buf[h] = vt
        sums = [
            dot_nn(vt[:, b * SUB : (b + 1) * SUB], k_buf[h, b * SUB : (b + 1) * SUB, :])
            for b in range(count)
        ]
        slot = 0
        while len(sums) > 1:
            for b in range(0, len(sums), 2):
                sub_buf[h, slot] = sums[b].astype(jnp.bfloat16)
                slot += 1
            sums = [sums[b] + sums[b + 1] for b in range(0, len(sums), 2)]
        state[h] = sums[0].astype(jnp.bfloat16)

    def first_sends(i):
        first_send(other(i)).start()

        @pl.when(core == 0)
        def _():
            first_send(mine(i)).start()

    def scaled(level, h, qt, lo, size):
        return (scale(level, h, lo, size) * qt).astype(jnp.bfloat16)

    def sibling(j, h):
        return jnp.where(bit(j) == 1, sib[j, h], jnp.zeros((DK, DK), jnp.bfloat16))

    def local(h):
        fetch(0, h).wait()
        qt_all = q_buf[h].T
        qt_buf[h] = qt_all
        s = lax.broadcasted_iota(jnp.int32, (SUB, SUB), 0)
        t = lax.broadcasted_iota(jnp.int32, (SUB, SUB), 1)
        causal = s <= t
        crossing = jnp.logical_and(s < STRETCH, t >= STRETCH)
        neighbour = sibling(0, h)
        for b in range(count):
            lo = b * SUB
            qt = qt_all[:, lo : lo + SUB]
            scores = dot_nn(k_buf[h, lo : lo + SUB, :], qt)
            weight = jnp.where(
                crossing, scale(1, h, lo, SUB), scale(0, h, lo, SUB)
            )
            weighted = jnp.where(causal, scores * weight, 0.0).astype(jnp.bfloat16)
            wide = qt.astype(jnp.float32)
            left = [vt_buf[h, :, lo : lo + SUB], neighbour]
            right = [weighted, scaled(1 + local_bits, h, wide, lo, SUB)]
            slot = 0
            for level in range(2, local_bits + 1):
                place = b >> (level - 2)
                if place % 2 == 1:
                    left.append(sub_buf[h, slot + place // 2])
                    right.append(scaled(level, h, wide, lo, SUB))
                slot += count >> (level - 1)
            out_t[h, :, lo : lo + SUB] = dot_nn(
                jnp.concatenate(left, axis=1), jnp.concatenate(right, axis=0)
            )

    def cross(group, h):
        wide = qt_buf[h].astype(jnp.float32)
        left = [sibling(j, h) for j in group]
        right = [scaled(1 + local_bits + j, h, wide, 0, rows) for j in group]
        return out_t[h] + dot_nn(jnp.concatenate(left, axis=1), jnp.concatenate(right, axis=0))

    def await_other(group, h):
        for j in group:
            guarded(bit(j) == 1, lambda: arrival(j, h).wait_recv())

    def middle(h):
        out_t[h] = cross(range(1, ctx_bits), h)

    def finish(h):
        out_buf[h] = cross(range(ctx_bits, depth), h).astype(jnp.bfloat16)
        put(h).start()

    def guarded(condition, action):
        if condition is None:
            action()
        else:
            pl.when(condition)(action)

    def sends(j):
        return bit(j) == 0 if j == last else None

    def receive(j, i):
        h = mine(i)
        guarded(bit(j) == 1 if j == last else None, lambda: arrival(j, h).wait_recv())
        if j >= 1:
            guarded(bit(j) == 1, lambda: forward(j, i).start())
        if j < last:
            held = state[h].astype(jnp.float32) if j == 0 else acc[i]
            total = held + sib[j, h].astype(jnp.float32)
            rounded = total.astype(jnp.bfloat16)
            run[j + 1, i] = rounded
            acc[i] = rounded.astype(jnp.float32) if j + 1 == ctx_bits else total
            guarded(sends(j + 1), lambda: stage_send(j + 1, i).start())

    block_sum(other(0))
    block_sum(mine(0))
    pl.semaphore_wait(barrier, depth)
    first_sends(0)

    def open_pair(i, carry):
        block_sum(other(i))
        block_sum(mine(i))
        first_sends(i)
        receive(0, i - 1)
        return carry

    lax.fori_loop(1, half, open_pair, 0)
    receive(0, half - 1)
    fetch_w().wait()
    for level in range(1 + local_bits + depth):
        for h in range(heads):
            w_head[h, level : level + 1, :] = w_buf[level, h : h + 1, :] * level_factor(level)

    lag = [0, 1, half] + [2 * half + 2 * j for j in range(depth - 3)]
    lag_middle = max(2 * half, lag[ctx_bits - 1] + 1)

    def between(i, low, high):
        return jnp.logical_and(i >= low, i < high)

    def wave(w, carry):
        for j in range(1, depth):
            i = w - lag[j]
            guarded(between(i, 0, half), functools.partial(receive, j, i))

        @pl.when(w < heads)
        def _():
            h = ((core + w) % 2) * half + w // 2

            @pl.when(jnp.logical_and(w % 2 == 1, bit(0) == 1))
            def _():
                arrival(0, h).wait_recv()

            local(h)

        i_middle = w - lag_middle

        @pl.when(between(i_middle, 0, half))
        def _():
            middle(mine(i_middle))
            await_other(range(1, ctx_bits), other(i_middle))
            middle(other(i_middle))

        final = w - lag[last]

        @pl.when(between(final, 0, half))
        def _():
            finish(mine(final))

        @pl.when(final >= 1)
        def _():
            await_other(range(ctx_bits, depth), other(final - 1))
            finish(other(final - 1))

        return carry

    lax.fori_loop(0, lag[last] + half + 1, wave, 0)

    def close(i, carry):
        first_send(other(i)).wait_send()
        guarded(core == 0, lambda: first_send(mine(i)).wait_send())
        for h in (mine(i), other(i)):
            put(h).wait()
        for j in range(1, depth):
            guarded(sends(j), lambda: stage_send(j, i).wait_send())
            guarded(bit(j) == 1, lambda: forward(j, i).wait_send())
        return carry

    lax.fori_loop(0, half, close, 0)


def on_device(ctx_count, grp_count, queries, keys, values, level_weights):
    rows = queries.shape[0]
    heads = level_weights.shape[1]
    count = rows // SUB
    ctx_bits = ctx_count.bit_length() - 1
    grp_bits = grp_count.bit_length() - 1
    depth = ctx_bits + grp_bits
    half = heads // 2
    bf16, f32 = jnp.bfloat16, jnp.float32
    any_spec = pl.BlockSpec(memory_space=pl.ANY)
    out = pl.pallas_call(
        functools.partial(kernel, ctx_bits, grp_bits),
        out_shape=jax.ShapeDtypeStruct((heads, DK, rows), bf16),
        in_specs=[pl.BlockSpec(memory_space=pltpu.HBM)] * 4,
        out_specs=any_spec,
        scratch_shapes=[
            pltpu.VMEM((heads, rows, DK), bf16),
            pltpu.VMEM((heads, rows, DK), bf16),
            pltpu.VMEM((heads, rows, DK), bf16),
            pltpu.VMEM(level_weights.shape, f32),
            pltpu.VMEM((heads, level_weights.shape[0], rows), f32),
            pltpu.VMEM((heads, DK, rows), bf16),
            pltpu.VMEM((heads, DK, rows), bf16),
            pltpu.VMEM((heads, count - 1, DK, DK), bf16),
            pltpu.VMEM((heads, DK, DK), bf16),
            pltpu.VMEM((depth, heads, DK, DK), bf16),
            pltpu.VMEM((depth, half, DK, DK), bf16),
            pltpu.VMEM((half, DK, DK), f32),
            pltpu.VMEM((heads, DK, rows), f32),
            pltpu.VMEM((heads, DK, rows), bf16),
            pltpu.SemaphoreType.DMA((3, heads)),
            pltpu.SemaphoreType.DMA,
            pltpu.SemaphoreType.DMA((heads,)),
            pltpu.SemaphoreType.DMA((depth, heads)),
            pltpu.SemaphoreType.DMA((depth, heads)),
            pltpu.SemaphoreType.DMA((depth, heads)),
        ],
        compiler_params=pltpu.CompilerParams(
            collective_id=0, has_side_effects=True, vmem_limit_bytes=60 * 2**20
        ),
        cost_estimate=pl.CostEstimate(
            flops=2 * rows * heads * DK * DK * (9 + depth), bytes_accessed=8 * rows * heads * DK,
            transcendentals=0,
        ),
    )(queries, keys, values, level_weights)
    return out.transpose(2, 0, 1).reshape(rows, heads * DK)


def solution(mesh):
    return jax.shard_map(
        functools.partial(on_device, mesh.shape["ctx"], mesh.shape["grp"]),
        mesh=mesh,
        in_specs=(
            P(("grp", "ctx"), None),
            P(("grp", "ctx"), None),
            P(("grp", "ctx"), None),
            P(None, None, ("grp", "ctx")),
        ),
        out_specs=P(("grp", "ctx"), None),
        check_vma=False,
    )
```

```python
import functools
import math

import jax
import jax.numpy as jnp
from jax import lax
from jax.experimental import pallas as pl
from jax.experimental.pallas import tpu as pltpu
from jax.sharding import PartitionSpec as P

DK = 128
STRETCH = 64
SUB = 2 * STRETCH
MESH = pl.DeviceIdType.MESH


def level_factor(level_num):
    token_count = STRETCH if level_num == 0 else STRETCH * 2 ** (level_num - 1)
    return 1.0 / math.sqrt(DK * token_count)


def dot_nt(a, b):
    return lax.dot_general(a, b, (((1,), (1,)), ((), ())), preferred_element_type=jnp.float32)


def dot_nn(a, b):
    return lax.dot_general(a, b, (((1,), (0,)), ((), ())), preferred_element_type=jnp.float32)


def kernel(
    ctx_bits, grp_bits,
    q_hbm, k_hbm, v_hbm, w_hbm, out_hbm,
    q_buf, k_buf, v_buf, w_buf, w_head, vt_buf, qt_buf, sub_buf, state, sib, run, acc, out_t, out_buf,
    in_sem, w_sem, out_sem, send_sem, fwd_sem, recv_sem,
):
    heads, rows = q_buf.shape[0], q_buf.shape[1]
    half = heads // 2
    count = rows // SUB
    local_bits = (rows // STRETCH).bit_length() - 1
    depth = ctx_bits + grp_bits
    last = depth - 1
    grp = lax.axis_index("grp")
    ctx = lax.axis_index("ctx")
    core = ctx % 2

    def bit(j):
        if j < ctx_bits:
            return (ctx // 2**j) % 2
        return (grp // 2 ** (j - ctx_bits)) % 2

    def partner(j):
        step = 1 - 2 * bit(j)
        if j < ctx_bits:
            return (grp, ctx + step * 2**j)
        return (grp + step * 2 ** (j - ctx_bits), ctx)

    def mine(i):
        return core * half + i

    def other(i):
        return (1 - core) * half + i

    def columns(h):
        return pl.ds(pl.multiple_of(h * DK, DK), DK)

    def fetch(n, h):
        src, dst = ((q_hbm, q_buf), (k_hbm, k_buf), (v_hbm, v_buf))[n]
        return pltpu.make_async_copy(src.at[:, columns(h)], dst.at[h], in_sem.at[n, h])

    def fetch_w():
        return pltpu.make_async_copy(w_hbm, w_buf, w_sem)

    def put(h):
        return pltpu.make_async_copy(out_buf.at[h], out_hbm.at[h], out_sem.at[h])

    def remote(src, j, h, sem, target):
        return pltpu.make_async_remote_copy(
            src_ref=src, dst_ref=sib.at[j, h], send_sem=sem, recv_sem=recv_sem.at[j, h],
            device_id=target, device_id_type=MESH,
        )

    def first_send(h):
        return remote(state.at[h], 0, h, send_sem.at[0, h], partner(0))

    def stage_send(j, i):
        return remote(run.at[j, i], j, mine(i), send_sem.at[j, mine(i)], partner(j))

    def forward(j, i):
        h = mine(i)
        return remote(sib.at[j, h], j, h, fwd_sem.at[j, h], partner(0))

    def arrival(j, h):
        return remote(sib.at[j, h], j, h, send_sem.at[j, h], partner(0))

    def scale(level, h, start, size):
        return w_head[h, level : level + 1, start : start + size]

    barrier = pltpu.get_barrier_semaphore()
    for i in range(half):
        for h in (other(i), mine(i)):
            fetch(1, h).start()
            fetch(2, h).start()
        if i == 0:
            for j in range(depth):
                pl.semaphore_signal(barrier, inc=1, device_id=partner(j), device_id_type=MESH)
    fetch_w().start()
    for i in range(half):
        for h in (mine(i), other(i)):
            fetch(0, h).start()

    def block_sum(h):
        fetch(1, h).wait()
        fetch(2, h).wait()
        vt = v_buf[h].T
        vt_buf[h] = vt
        sums = [
            dot_nn(vt[:, b * SUB : (b + 1) * SUB], k_buf[h, b * SUB : (b + 1) * SUB, :])
            for b in range(count)
        ]
        slot = 0
        while len(sums) > 1:
            for b in range(0, len(sums), 2):
                sub_buf[h, slot] = sums[b].astype(jnp.bfloat16)
                slot += 1
            sums = [sums[b] + sums[b + 1] for b in range(0, len(sums), 2)]
        state[h] = sums[0].astype(jnp.bfloat16)

    def first_sends(i):
        first_send(other(i)).start()

        @pl.when(core == 0)
        def _():
            first_send(mine(i)).start()

    def scaled(level, h, qt, lo, size):
        return (scale(level, h, lo, size) * qt).astype(jnp.bfloat16)

    def sibling(j, h):
        return jnp.where(bit(j) == 1, sib[j, h], jnp.zeros((DK, DK), jnp.bfloat16))

    def local(h):
        fetch(0, h).wait()
        qt_all = q_buf[h].T
        qt_buf[h] = qt_all
        s = lax.broadcasted_iota(jnp.int32, (SUB, SUB), 0)
        t = lax.broadcasted_iota(jnp.int32, (SUB, SUB), 1)
        causal = s <= t
        crossing = jnp.logical_and(s < STRETCH, t >= STRETCH)
        neighbour = sibling(0, h)
        for b in range(count):
            lo = b * SUB
            qt = qt_all[:, lo : lo + SUB]
            scores = dot_nn(k_buf[h, lo : lo + SUB, :], qt)
            weight = jnp.where(
                crossing, scale(1, h, lo, SUB), scale(0, h, lo, SUB)
            )
            weighted = jnp.where(causal, scores * weight, 0.0).astype(jnp.bfloat16)
            wide = qt.astype(jnp.float32)
            left = [vt_buf[h, :, lo : lo + SUB], neighbour]
            right = [weighted, scaled(1 + local_bits, h, wide, lo, SUB)]
            slot = 0
            for level in range(2, local_bits + 1):
                place = b >> (level - 2)
                if place % 2 == 1:
                    left.append(sub_buf[h, slot + place // 2])
                    right.append(scaled(level, h, wide, lo, SUB))
                slot += count >> (level - 1)
            out_t[h, :, lo : lo + SUB] = dot_nn(
                jnp.concatenate(left, axis=1), jnp.concatenate(right, axis=0)
            )

    def cross(group, h):
        wide = qt_buf[h].astype(jnp.float32)
        left = [sibling(j, h) for j in group]
        right = [scaled(1 + local_bits + j, h, wide, 0, rows) for j in group]
        return out_t[h] + dot_nn(jnp.concatenate(left, axis=1), jnp.concatenate(right, axis=0))

    def await_other(group, h):
        for j in group:
            guarded(bit(j) == 1, lambda: arrival(j, h).wait_recv())

    def middle(h):
        out_t[h] = cross(range(1, ctx_bits), h)

    def finish(h):
        out_buf[h] = cross(range(ctx_bits, depth), h).astype(jnp.bfloat16)
        put(h).start()

    def guarded(condition, action):
        if condition is None:
            action()
        else:
            pl.when(condition)(action)

    def sends(j):
        return bit(j) == 0 if j == last else None

    def receive(j, i):
        h = mine(i)
        guarded(bit(j) == 1 if j == last else None, lambda: arrival(j, h).wait_recv())
        if j >= 1:
            guarded(bit(j) == 1, lambda: forward(j, i).start())
        if j < last:
            held = state[h].astype(jnp.float32) if j == 0 else acc[i]
            total = held + sib[j, h].astype(jnp.float32)
            rounded = total.astype(jnp.bfloat16)
            run[j + 1, i] = rounded
            acc[i] = rounded.astype(jnp.float32) if j + 1 == ctx_bits else total
            guarded(sends(j + 1), lambda: stage_send(j + 1, i).start())

    block_sum(other(0))
    block_sum(mine(0))
    pl.semaphore_wait(barrier, depth)
    first_sends(0)

    def open_pair(i, carry):
        block_sum(other(i))
        block_sum(mine(i))
        first_sends(i)
        receive(0, i - 1)
        return carry

    lax.fori_loop(1, half, open_pair, 0)
    receive(0, half - 1)
    fetch_w().wait()
    for level in range(1 + local_bits + depth):
        for h in range(heads):
            w_head[h, level : level + 1, :] = w_buf[level, h : h + 1, :] * level_factor(level)

    lag = [0, 1, half] + [2 * half + 2 * j for j in range(depth - 3)]
    lag_middle = max(2 * half, lag[ctx_bits - 1] + 1)

    def between(i, low, high):
        return jnp.logical_and(i >= low, i < high)

    def wave(w, carry):
        for j in range(1, depth):
            i = w - lag[j]
            guarded(between(i, 0, half), functools.partial(receive, j, i))

        @pl.when(w < heads)
        def _():
            h = ((core + w) % 2) * half + w // 2

            @pl.when(jnp.logical_and(w % 2 == 1, bit(0) == 1))
            def _():
                arrival(0, h).wait_recv()

            local(h)

        i_middle = w - lag_middle

        @pl.when(between(i_middle, 0, half))
        def _():
            middle(mine(i_middle))
            await_other(range(1, ctx_bits), other(i_middle))
            middle(other(i_middle))

        final = w - lag[last]

        @pl.when(between(final, 0, half))
        def _():
            finish(mine(final))

        @pl.when(final >= 1)
        def _():
            await_other(range(ctx_bits, depth), other(final - 1))
            finish(other(final - 1))

        return carry

    lax.fori_loop(0, lag[last] + half + 1, wave, 0)

    def close(i, carry):
        first_send(other(i)).wait_send()
        guarded(core == 0, lambda: first_send(mine(i)).wait_send())
        for h in (mine(i), other(i)):
            put(h).wait()
        for j in range(1, depth):
            guarded(sends(j), lambda: stage_send(j, i).wait_send())
            guarded(bit(j) == 1, lambda: forward(j, i).wait_send())
        return carry

    lax.fori_loop(0, half, close, 0)


def on_device(ctx_count, grp_count, queries, keys, values, level_weights):
    rows = queries.shape[0]
    heads = level_weights.shape[1]
    count = rows // SUB
    ctx_bits = ctx_count.bit_length() - 1
    grp_bits = grp_count.bit_length() - 1
    depth = ctx_bits + grp_bits
    half = heads // 2
    bf16, f32 = jnp.bfloat16, jnp.float32
    any_spec = pl.BlockSpec(memory_space=pl.ANY)
    out = pl.pallas_call(
        functools.partial(kernel, ctx_bits, grp_bits),
        out_shape=jax.ShapeDtypeStruct((heads, DK, rows), bf16),
        in_specs=[pl.BlockSpec(memory_space=pltpu.HBM)] * 4,
        out_specs=any_spec,
        scratch_shapes=[
            pltpu.VMEM((heads, rows, DK), bf16),
            pltpu.VMEM((heads, rows, DK), bf16),
            pltpu.VMEM((heads, rows, DK), bf16),
            pltpu.VMEM(level_weights.shape, f32),
            pltpu.VMEM((heads, level_weights.shape[0], rows), f32),
            pltpu.VMEM((heads, DK, rows), bf16),
            pltpu.VMEM((heads, DK, rows), bf16),
            pltpu.VMEM((heads, count - 1, DK, DK), bf16),
            pltpu.VMEM((heads, DK, DK), bf16),
            pltpu.VMEM((depth, heads, DK, DK), bf16),
            pltpu.VMEM((depth, half, DK, DK), bf16),
            pltpu.VMEM((half, DK, DK), f32),
            pltpu.VMEM((heads, DK, rows), f32),
            pltpu.VMEM((heads, DK, rows), bf16),
            pltpu.SemaphoreType.DMA((3, heads)),
            pltpu.SemaphoreType.DMA,
            pltpu.SemaphoreType.DMA((heads,)),
            pltpu.SemaphoreType.DMA((depth, heads)),
            pltpu.SemaphoreType.DMA((depth, heads)),
            pltpu.SemaphoreType.DMA((depth, heads)),
        ],
        compiler_params=pltpu.CompilerParams(
            collective_id=0, has_side_effects=True, vmem_limit_bytes=52 * 2**20
        ),
        cost_estimate=pl.CostEstimate(
            flops=2 * rows * heads * DK * DK * (9 + depth), bytes_accessed=8 * rows * heads * DK,
            transcendentals=0,
        ),
    )(queries, keys, values, level_weights)
    return out.transpose(2, 0, 1).reshape(rows, heads * DK)


def solution(mesh):
    return jax.shard_map(
        functools.partial(on_device, mesh.shape["ctx"], mesh.shape["grp"]),
        mesh=mesh,
        in_specs=(
            P(("grp", "ctx"), None),
            P(("grp", "ctx"), None),
            P(("grp", "ctx"), None),
            P(None, None, ("grp", "ctx")),
        ),
        out_specs=P(("grp", "ctx"), None),
        check_vma=False,
    )
```

```python
import functools
import math

import jax
import jax.numpy as jnp
from jax import lax
from jax.experimental import pallas as pl
from jax.experimental.pallas import tpu as pltpu
from jax.sharding import PartitionSpec as P

DK = 128
STRETCH = 64
SUB = 2 * STRETCH
MESH = pl.DeviceIdType.MESH


def level_factor(level_num):
    token_count = STRETCH if level_num == 0 else STRETCH * 2 ** (level_num - 1)
    return 1.0 / math.sqrt(DK * token_count)


def dot_nt(a, b):
    return lax.dot_general(a, b, (((1,), (1,)), ((), ())), preferred_element_type=jnp.float32)


def dot_nn(a, b):
    return lax.dot_general(a, b, (((1,), (0,)), ((), ())), preferred_element_type=jnp.float32)


def kernel(
    ctx_bits, grp_bits,
    q_hbm, k_hbm, v_hbm, w_hbm, out_hbm,
    q_buf, k_buf, v_buf, w_buf, w_head, vt_buf, qt_buf, sub_buf, state, sib, run, acc, out_t, out_buf,
    in_sem, w_sem, out_sem, send_sem, fwd_sem, recv_sem,
):
    heads, rows = q_buf.shape[0], q_buf.shape[1]
    half = heads // 2
    count = rows // SUB
    local_bits = (rows // STRETCH).bit_length() - 1
    depth = ctx_bits + grp_bits
    last = depth - 1
    grp = lax.axis_index("grp")
    ctx = lax.axis_index("ctx")
    core = ctx % 2

    def bit(j):
        if j < ctx_bits:
            return (ctx // 2**j) % 2
        return (grp // 2 ** (j - ctx_bits)) % 2

    def partner(j):
        step = 1 - 2 * bit(j)
        if j < ctx_bits:
            return (grp, ctx + step * 2**j)
        return (grp + step * 2 ** (j - ctx_bits), ctx)

    def mine(i):
        return core * half + i

    def other(i):
        return (1 - core) * half + i

    def columns(h):
        return pl.ds(pl.multiple_of(h * DK, DK), DK)

    def fetch(n, h):
        src, dst = ((q_hbm, q_buf), (k_hbm, k_buf), (v_hbm, v_buf))[n]
        return pltpu.make_async_copy(src.at[:, columns(h)], dst.at[h], in_sem.at[n, h])

    def fetch_w():
        return pltpu.make_async_copy(w_hbm, w_buf, w_sem)

    def put(h):
        return pltpu.make_async_copy(out_buf.at[h], out_hbm.at[h], out_sem.at[h])

    def remote(src, j, h, sem, target):
        return pltpu.make_async_remote_copy(
            src_ref=src, dst_ref=sib.at[j, h], send_sem=sem, recv_sem=recv_sem.at[j, h],
            device_id=target, device_id_type=MESH,
        )

    def first_send(h):
        return remote(state.at[h], 0, h, send_sem.at[0, h], partner(0))

    def stage_send(j, i):
        return remote(run.at[j, i], j, mine(i), send_sem.at[j, mine(i)], partner(j))

    def forward(j, i):
        h = mine(i)
        return remote(sib.at[j, h], j, h, fwd_sem.at[j, h], partner(0))

    def arrival(j, h):
        return remote(sib.at[j, h], j, h, send_sem.at[j, h], partner(0))

    def scale(level, h, start, size):
        return w_head[h, level : level + 1, start : start + size]

    barrier = pltpu.get_barrier_semaphore()
    for i in range(half):
        for h in (other(i), mine(i)):
            fetch(1, h).start()
            fetch(2, h).start()
        if i == 0:
            for j in range(depth):
                pl.semaphore_signal(barrier, inc=1, device_id=partner(j), device_id_type=MESH)
    fetch_w().start()
    for i in range(half):
        for h in (mine(i), other(i)):
            fetch(0, h).start()

    def block_sum(h):
        fetch(1, h).wait()
        fetch(2, h).wait()
        vt = v_buf[h].T
        vt_buf[h] = vt
        sums = [
            dot_nn(vt[:, b * SUB : (b + 1) * SUB], k_buf[h, b * SUB : (b + 1) * SUB, :])
            for b in range(count)
        ]
        slot = 0
        while len(sums) > 1:
            for b in range(0, len(sums), 2):
                sub_buf[h, slot] = sums[b].astype(jnp.bfloat16)
                slot += 1
            sums = [sums[b] + sums[b + 1] for b in range(0, len(sums), 2)]
        state[h] = sums[0].astype(jnp.bfloat16)

    def first_sends(i):
        first_send(other(i)).start()

        @pl.when(core == 0)
        def _():
            first_send(mine(i)).start()

    def scaled(level, h, qt, lo, size):
        return (scale(level, h, lo, size) * qt).astype(jnp.bfloat16)

    def sibling(j, h):
        return jnp.where(bit(j) == 1, sib[j, h], jnp.zeros((DK, DK), jnp.bfloat16))

    def local(h):
        fetch(0, h).wait()
        qt_all = q_buf[h].T
        qt_buf[h] = qt_all
        s = lax.broadcasted_iota(jnp.int32, (SUB, SUB), 0)
        t = lax.broadcasted_iota(jnp.int32, (SUB, SUB), 1)
        causal = s <= t
        crossing = jnp.logical_and(s < STRETCH, t >= STRETCH)
        neighbour = sibling(0, h)
        for b in range(count):
            lo = b * SUB
            qt = qt_all[:, lo : lo + SUB]
            scores = dot_nn(k_buf[h, lo : lo + SUB, :], qt)
            weight = jnp.where(
                crossing, scale(1, h, lo, SUB), scale(0, h, lo, SUB)
            )
            weighted = jnp.where(causal, scores * weight, 0.0).astype(jnp.bfloat16)
            wide = qt.astype(jnp.float32)
            left = [vt_buf[h, :, lo : lo + SUB], neighbour]
            right = [weighted, scaled(1 + local_bits, h, wide, lo, SUB)]
            slot = 0
            for level in range(2, local_bits + 1):
                place = b >> (level - 2)
                if place % 2 == 1:
                    left.append(sub_buf[h, slot + place // 2])
                    right.append(scaled(level, h, wide, lo, SUB))
                slot += count >> (level - 1)
            out_t[h, :, lo : lo + SUB] = dot_nn(
                jnp.concatenate(left, axis=1), jnp.concatenate(right, axis=0)
            )

    def cross(group, h):
        wide = qt_buf[h].astype(jnp.float32)
        left = [sibling(j, h) for j in group]
        right = [scaled(1 + local_bits + j, h, wide, 0, rows) for j in group]
        return out_t[h] + dot_nn(jnp.concatenate(left, axis=1), jnp.concatenate(right, axis=0))

    def await_other(group, h):
        for j in group:
            guarded(bit(j) == 1, lambda: arrival(j, h).wait_recv())

    def middle(h):
        out_t[h] = cross(range(1, ctx_bits), h)

    def finish(h):
        out_buf[h] = cross(range(ctx_bits, depth), h).astype(jnp.bfloat16)
        put(h).start()

    def guarded(condition, action):
        if condition is None:
            action()
        else:
            pl.when(condition)(action)

    def sends(j):
        return bit(j) == 0 if j == last else None

    def receive(j, i):
        h = mine(i)
        guarded(bit(j) == 1 if j == last else None, lambda: arrival(j, h).wait_recv())
        if j >= 1:
            guarded(bit(j) == 1, lambda: forward(j, i).start())
        if j < last:
            held = state[h].astype(jnp.float32) if j == 0 else acc[i]
            total = held + sib[j, h].astype(jnp.float32)
            rounded = total.astype(jnp.bfloat16)
            run[j + 1, i] = rounded
            acc[i] = rounded.astype(jnp.float32) if j + 1 == ctx_bits else total
            guarded(sends(j + 1), lambda: stage_send(j + 1, i).start())

    block_sum(other(0))
    block_sum(mine(0))
    pl.semaphore_wait(barrier, depth)
    first_sends(0)

    def open_pair(i, carry):
        block_sum(other(i))
        block_sum(mine(i))
        first_sends(i)
        receive(0, i - 1)
        return carry

    lax.fori_loop(1, half, open_pair, 0)
    fetch_w().wait()
    for level in range(1 + local_bits + depth):
        for h in range(heads):
            w_head[h, level : level + 1, :] = w_buf[level, h : h + 1, :] * level_factor(level)

    receive(0, half - 1)
    lag = [0] + [1 + 2 * j for j in range(depth - 1)]
    lag_middle = max(half + 2, lag[ctx_bits - 1] + 1)

    def between(i, low, high):
        return jnp.logical_and(i >= low, i < high)

    def wave(w, carry):
        for j in range(1, depth):
            i = w - lag[j]
            guarded(between(i, 0, half), functools.partial(receive, j, i))

        @pl.when(w < heads)
        def _():
            h = ((core + w) % 2) * half + w // 2

            @pl.when(jnp.logical_and(w % 2 == 1, bit(0) == 1))
            def _():
                arrival(0, h).wait_recv()

            local(h)

        i_middle = w - lag_middle

        @pl.when(between(i_middle, 0, half))
        def _():
            middle(mine(i_middle))
            await_other(range(1, ctx_bits), other(i_middle))
            middle(other(i_middle))

        final = w - lag[last]

        @pl.when(between(final, 0, half))
        def _():
            finish(mine(final))

        @pl.when(final >= 1)
        def _():
            await_other(range(ctx_bits, depth), other(final - 1))
            finish(other(final - 1))

        return carry

    lax.fori_loop(0, lag[last] + half + 1, wave, 0)

    def close(i, carry):
        first_send(other(i)).wait_send()
        guarded(core == 0, lambda: first_send(mine(i)).wait_send())
        for h in (mine(i), other(i)):
            put(h).wait()
        for j in range(1, depth):
            guarded(sends(j), lambda: stage_send(j, i).wait_send())
            guarded(bit(j) == 1, lambda: forward(j, i).wait_send())
        return carry

    lax.fori_loop(0, half, close, 0)


def on_device(ctx_count, grp_count, queries, keys, values, level_weights):
    rows = queries.shape[0]
    heads = level_weights.shape[1]
    count = rows // SUB
    ctx_bits = ctx_count.bit_length() - 1
    grp_bits = grp_count.bit_length() - 1
    depth = ctx_bits + grp_bits
    half = heads // 2
    bf16, f32 = jnp.bfloat16, jnp.float32
    any_spec = pl.BlockSpec(memory_space=pl.ANY)
    out = pl.pallas_call(
        functools.partial(kernel, ctx_bits, grp_bits),
        out_shape=jax.ShapeDtypeStruct((heads, DK, rows), bf16),
        in_specs=[pl.BlockSpec(memory_space=pltpu.HBM)] * 4,
        out_specs=any_spec,
        scratch_shapes=[
            pltpu.VMEM((heads, rows, DK), bf16),
            pltpu.VMEM((heads, rows, DK), bf16),
            pltpu.VMEM((heads, rows, DK), bf16),
            pltpu.VMEM(level_weights.shape, f32),
            pltpu.VMEM((heads, level_weights.shape[0], rows), f32),
            pltpu.VMEM((heads, DK, rows), bf16),
            pltpu.VMEM((heads, DK, rows), bf16),
            pltpu.VMEM((heads, count - 1, DK, DK), bf16),
            pltpu.VMEM((heads, DK, DK), bf16),
            pltpu.VMEM((depth, heads, DK, DK), bf16),
            pltpu.VMEM((depth, half, DK, DK), bf16),
            pltpu.VMEM((half, DK, DK), f32),
            pltpu.VMEM((heads, DK, rows), f32),
            pltpu.VMEM((heads, DK, rows), bf16),
            pltpu.SemaphoreType.DMA((3, heads)),
            pltpu.SemaphoreType.DMA,
            pltpu.SemaphoreType.DMA((heads,)),
            pltpu.SemaphoreType.DMA((depth, heads)),
            pltpu.SemaphoreType.DMA((depth, heads)),
            pltpu.SemaphoreType.DMA((depth, heads)),
        ],
        compiler_params=pltpu.CompilerParams(
            collective_id=0, has_side_effects=True, vmem_limit_bytes=60 * 2**20
        ),
        cost_estimate=pl.CostEstimate(
            flops=2 * rows * heads * DK * DK * (9 + depth), bytes_accessed=8 * rows * heads * DK,
            transcendentals=0,
        ),
    )(queries, keys, values, level_weights)
    return out.transpose(2, 0, 1).reshape(rows, heads * DK)


def solution(mesh):
    return jax.shard_map(
        functools.partial(on_device, mesh.shape["ctx"], mesh.shape["grp"]),
        mesh=mesh,
        in_specs=(
            P(("grp", "ctx"), None),
            P(("grp", "ctx"), None),
            P(("grp", "ctx"), None),
            P(None, None, ("grp", "ctx")),
        ),
        out_specs=P(("grp", "ctx"), None),
        check_vma=False,
    )
```
